512 devices in a mesh: blk: 128 (over y, z, core), face: 4 (over x).
Axes of the slice: x: 4, y: 4, z: 16, core: 2. Of those that a mesh axis runs over, the one named last changes fastest.
Arguments:
- flow_state: float32 [6, 16, 512, 1024], P(None, None, 'blk', 'face'), may hold values from -6 to 6
- viscosity: float32 [16, 512, 1024], P(None, 'blk', 'face'), may hold values from 0.03 to 0.15
- flux_jacobians: float32 [3, 6, 6], replicated, may hold values from -0.9 to 0.9
- rbf_weights: float32 [8, 24, 65536], P(None, None, ('blk', 'face')), may hold values from -1.25 to 1.25
- rbf_columns: int32 [4, 65536], P(None, ('blk', 'face')), may hold values from 0 to 255
- patch_owner: int32 [65536, 1], P(('blk', 'face')), may hold values from 0 to 127; in each aligned block of 128 rows (0 to 127, 128 to 255, ...) at most 8 rows name the same one
- stiff_blocks: float32 [8, 6, 6, 32768], P(None, None, None, 'blk'), as said below
- stiff_columns: int32 [8, 32768], P(None, 'blk'), may hold values from 0 to 511, as said below
Outputs:
- flow_out: float32 [6, 16, 512, 1024], P(None, None, 'blk', 'face')
- shell_motion: float32 [6, 32768], P(None, 'blk')
- surface_motion: float32 [8, 65536], P(None, ('blk', 'face'))
The draws below stay inside these ranges and needn't reach their ends.
Inputs may be any that keep to these rules, and one draw needn't show every extreme that they name: `patch_owner`: among the patches of one device no owner is named more than 8 times, a bound that some block reaches. `stiff_columns`: block 0 and block 7 of node m point to m itself, block 7 being zero; the others come in pairs at node offsets +s and -s, one pair with s = 128, the same offsets for every node; K is symmetric and positive definite. `stiff_blocks`: K is symmetric and positive definite.
All inputs are finite; a program needn't handle non-finite values.
Results may differ from the reference program's by a relative error of at most 0.0003.
Values sent between devices are 32-bit elements; how exact they have to be, the bound alone decides.
A program may use at most 64 MiB of HBM per device.

```python
import math
import jax
import jax.numpy as jnp
import numpy as np
from jax import lax

NV = 6
CN = 16
CS = 4
CC = 256
PP = 8
KR = 4
DOF = 6
NN = 256
HB = 128
NBR = 8
ITERS_CFD = 2
CG_ITERS = 4
NP = 128
CAP = 8
SPAN = 512
CHORD = 1024
PATCHES = 65536
NODES = 32768
N_BLK = 128
N_FACE = 4


def band_offsets(key):
    picked = jax.random.permutation(key, HB - 1)[:2] + 1
    return picked.astype(jnp.int32)


def draw_stiff_columns(key, part):
    picked = band_offsets(key)
    zero_slot = jnp.zeros((1,), jnp.int32)
    far_reach = jnp.full((1,), HB, jnp.int32)
    offsets = jnp.concatenate([zero_slot, far_reach, -far_reach, picked[0:1], -picked[0:1], picked[1:2], -picked[1:2], zero_slot])
    local_index = jnp.arange(NODES, dtype=jnp.int32) % NN
    return local_index[None, :] + HB + offsets[:, None]


def draw_stiff_blocks(key, part):
    picked = band_offsets(key)
    key = jax.random.fold_in(key, 7)
    subkeys = jax.random.split(key, 5)
    identity = jnp.eye(DOF, dtype=jnp.float32)[:, :, None]
    reaches = [HB, picked[0], picked[1]]
    couplings = []
    diagonal = jnp.zeros((DOF, DOF, NODES), jnp.float32)
    for member in range(3):
        raw = jax.random.uniform(subkeys[member + 1], (DOF, DOF, NODES), jnp.float32, -0.02, 0.02)
        bond = 0.14 * identity + 0.5 * (raw + raw.transpose(1, 0, 2))
        bond_back = jnp.roll(bond, reaches[member], axis=2)
        couplings.append(-bond)
        couplings.append(-bond_back.transpose(1, 0, 2))
        diagonal = diagonal + bond + bond_back
    settle = jax.random.uniform(subkeys[0], (NODES,), jnp.float32, 0.005, 0.02)
    diagonal = diagonal + identity * settle[None, None, :]
    blocks = [diagonal] + couplings + [jnp.zeros((DOF, DOF, NODES), jnp.float32)]
    return jnp.stack(blocks)


def with_ends(values, stream_key, smallest, largest):
    longest = values.shape.index(max(values.shape))
    spots = []
    for shift in (0, 1):
        where = [jax.random.randint(jax.random.fold_in(stream_key, axis), (), 0, length) for axis, length in enumerate(values.shape)]
        where[longest] = (where[longest] + shift) % values.shape[longest]
        spots.append(tuple(where))
    return values.at[spots[0]].set(smallest).at[spots[1]].set(largest)


def block_levels(own_key, dims, shards, least, top_value):
    loudness = 1.0
    for dim, blocks in shards:
        steps = jax.random.uniform(jax.random.fold_in(jax.random.fold_in(own_key, 6), dim), (blocks,), jnp.float32, least / len(shards), top_value / len(shards))
        loudness = loudness * jnp.repeat(jnp.exp(steps), dims[dim] // blocks).reshape((-1,) + (1,) * (len(dims) - 1 - dim))
    return loudness


def routed_block(own_key, own, number, rows, number_of, top, limit, slope):
    sequence = jax.random.permutation(own_key, number_of)
    crowded, usual = shares(number_of, rows * top, limit, slope, True), shares(number_of, rows * top, limit, slope, False)
    places = jnp.arange(number_of)

    def named(tallies, offset_by):
        used = int((tallies > 0).sum())
        fixed = max(1, used // 4)
        moved = fixed + (places - fixed + offset_by * (used - fixed)) % max(1, number_of - fixed)
        return jnp.zeros((number_of,), jnp.int32).at[sequence[jnp.where(places < fixed, places, moved)]].set(jnp.asarray(tallies, jnp.int32))

    tallies = jnp.where(number % 4 == 0, named(crowded, number // 4), named(usual, number - number // 4 - 1))
    mixed = jax.random.permutation(jax.random.fold_in(own, 3), number_of)
    giver, taker = mixed[0:number_of // 2 * 2:2], mixed[1:number_of // 2 * 2:2]
    margin = jnp.minimum(tallies[giver] - 1, limit - tallies[taker]) // 2
    margin = jnp.where((giver == sequence[0]) | (taker == sequence[0]) | (tallies[taker] == 0), 0, jnp.maximum(margin, 0))
    moved = jax.random.randint(jax.random.fold_in(own, 4), (number_of // 2,), 0, 1 << 20) % (margin + 1)
    tallies = tallies.at[giver].add(-moved).at[taker].add(moved)
    members = jnp.searchsorted(jnp.cumsum(tallies), jnp.arange(rows * top), side="right").astype(jnp.int32)
    table = members.reshape(top, rows).T
    table = table[jax.random.permutation(jax.random.fold_in(own, 1), rows)]
    offset_by = jax.random.randint(jax.random.fold_in(own, 2), (rows, 1), 0, top)
    return jnp.take_along_axis(table, (jnp.arange(top)[None, :] + offset_by) % top, axis=1)


def shares(count, total, limit, slope, full):
    weights = [(1 << 20) // math.isqrt(standing ** slope) + 1 for standing in range(1, count + 1)]
    largest = limit if full else min(limit, max(-(-total // count), total * weights[0] // sum(weights)))
    least = 1 if total - largest >= count - 1 else 0
    given, spare = [largest] + [least] * (count - 1), total - largest - least * (count - 1)
    while spare > 0:
        free = [i for i in range(1, count) if given[i] < largest] or [i for i in range(1, count) if given[i] < limit]
        whole, left = sum([weights[i] for i in free]), spare
        for i in free:
            more = min(limit - given[i], max(1, left * weights[i] // whole), spare)
            given[i] = given[i] + more
            spare = spare - more
    return np.array(given)


def centred(stream_key, extent, scale, bound, cuts=(), kind=jnp.bfloat16):
    entries = scale * jax.random.normal(stream_key, extent, jnp.float32)
    if cuts:
        entries = entries * block_levels(stream_key, extent, cuts, -0.22, 0.18)
    return jnp.clip(entries, -bound, bound).astype(kind)


def setup_inputs(seed: int = 0) -> dict:
    key_of = jax.random.split(jax.random.key(seed), 9)
    flow_state = centred(key_of[0], (NV, CN, SPAN, CHORD), 1.0, 6.0, ((2, 128), (3, 4)), jnp.float32)
    viscosity = jnp.clip(jnp.exp(math.log(0.15) - 1.609438 * jax.random.uniform(key_of[1], (CN, SPAN, CHORD), jnp.float32) ** block_levels(key_of[1], (CN, SPAN, CHORD), ((1, 128), (2, 4)), -0.2, 0.2)), 0.03, 0.15)
    flux_jacobians = centred(key_of[2], (3, NV, NV), 0.15, 0.9, (), jnp.float32)
    rbf_weights = centred(key_of[3], (PP, KR * DOF, PATCHES), (KR * DOF) ** -0.5, 1.25, ((2, 512),), jnp.float32)
    rbf_columns = with_ends(jax.random.randint(key_of[4], (KR, PATCHES), 0, NN), jax.random.fold_in(key_of[4], 1), 0, NN - 1).astype(jnp.int32)
    patch_owner_keys = jax.random.split(jax.random.fold_in(key_of[5], 1), PATCHES // NP)
    patch_owner_turns = jax.random.permutation(jax.random.fold_in(key_of[5], 3), PATCHES // NP)
    patch_owner = jax.vmap(lambda own, number: routed_block(jax.random.fold_in(key_of[5], 2), own, number, NP, N_BLK, 1, CAP, 2))(patch_owner_keys, patch_owner_turns).reshape((PATCHES, 1))
    stiff_blocks = draw_stiff_blocks(jax.random.fold_in(key_of[8], 71), 0)
    stiff_columns = draw_stiff_columns(jax.random.fold_in(key_of[8], 71), 0)
    return dict(flow_state=flow_state, viscosity=viscosity, flux_jacobians=flux_jacobians, rbf_weights=rbf_weights, rbf_columns=rbf_columns, patch_owner=patch_owner, stiff_blocks=stiff_blocks, stiff_columns=stiff_columns)


HIGH = lax.Precision.HIGHEST


def relaxation(padded, viscosity, flux_jacobians):
    centre = padded[:, 1:-1, 1:-1, 1:-1]
    neighbours = ((padded[:, 2:, 1:-1, 1:-1], padded[:, :-2, 1:-1, 1:-1]),
                  (padded[:, 1:-1, 2:, 1:-1], padded[:, 1:-1, :-2, 1:-1]),
                  (padded[:, 1:-1, 1:-1, 2:], padded[:, 1:-1, 1:-1, :-2]))
    spread = -6.0 * centre
    transport = jnp.zeros_like(centre)
    for axis_id in range(3):
        higher_side, lower_side = neighbours[axis_id]
        spread = spread + higher_side + lower_side
        transport = transport + jnp.einsum("ij,jabc->iabc", flux_jacobians[axis_id], 0.5 * (higher_side - lower_side), precision=HIGH)
    return centre - transport + viscosity[None] * spread


def take_rows(block_rows, block_cols):
    return block_rows[:, block_cols]


def stiffness_all(vector, stiff_blocks, stiff_columns):
    parts = vector.reshape(DOF, N_BLK, NN)
    zeros_rim = jnp.zeros((DOF, 1, HB), vector.dtype)
    left_rim = jnp.concatenate([zeros_rim, parts[:, :-1, NN - HB:]], axis=1)
    right_rim = jnp.concatenate([parts[:, 1:, :HB], zeros_rim], axis=1)
    widened = jnp.concatenate([left_rim, parts, right_rim], axis=2)
    columns = stiff_columns.reshape(NBR, N_BLK, NN)
    taken = jax.vmap(take_rows, in_axes=(1, 1), out_axes=2)(widened, columns)
    taken = taken.reshape(DOF, NBR, NODES)
    return jnp.einsum("jcdn,djn->cn", stiff_blocks, taken, precision=HIGH)


def reference(flow_state, viscosity, flux_jacobians, rbf_weights, rbf_columns, patch_owner, stiff_blocks, stiff_columns):
    state = flow_state
    for sweep_index in range(ITERS_CFD):
        padded = jnp.pad(state, ((0, 0), (1, 1), (1, 1), (1, 1)))
        state = relaxation(padded, viscosity, flux_jacobians)
    wall = state[0, 0]
    pressure = wall.reshape(N_BLK, CS, N_FACE, CC // PP, PP).transpose(4, 0, 2, 1, 3).reshape(PP, PATCHES)
    loads = jnp.einsum("pkn,pn->kn", rbf_weights, pressure, precision=HIGH)
    global_nodes = patch_owner[:, 0][None, :] * NN + rbf_columns
    contrib = loads.reshape(KR, DOF, PATCHES).transpose(0, 2, 1).reshape(KR * PATCHES, DOF)
    force = jax.ops.segment_sum(contrib, global_nodes.reshape(-1), num_segments=NODES).T
    solution = jnp.zeros_like(force)
    residual = force
    direction = force
    norm_now = jnp.sum(residual * residual)
    for sweep_index in range(CG_ITERS):
        image = stiffness_all(direction, stiff_blocks, stiff_columns)
        alpha = norm_now / jnp.sum(direction * image)
        solution = solution + alpha * direction
        residual = residual - alpha * image
        norm_next = jnp.sum(residual * residual)
        direction = residual + (norm_next / norm_now) * direction
        norm_now = norm_next
    gathered = solution[:, global_nodes]
    node_values = gathered.transpose(1, 0, 2).reshape(KR * DOF, PATCHES)
    motion = jnp.einsum("pkn,kn->pn", rbf_weights, node_values, precision=HIGH)
    return state, solution, motion
```

```python
import functools

import jax
import jax.numpy as jnp
from jax import lax
from jax.experimental import pallas as pl
from jax.experimental.pallas import tpu as pltpu
from jax.sharding import PartitionSpec as P

MESH = pl.DeviceIdType.MESH
F32 = jnp.float32
BF16 = jnp.bfloat16
DOF = 6
WALL = 3
CORES = 2
REACH = 2


def iota(shape, dim):
    return lax.broadcasted_iota(jnp.int32, shape, dim)


def three_parts(x):
    high = x.astype(BF16).astype(F32)
    rest = x - high
    middle = rest.astype(BF16).astype(F32)
    return high, middle, rest - middle


def stacked_parts(x):
    return jnp.concatenate(three_parts(x), axis=0)


def exact_dot(x, table, dims):
    rows = x.shape[0]
    out = lax.dot_general(
        stacked_parts(x).astype(BF16), table, (dims, ((), ())), preferred_element_type=F32
    )
    return out[:rows] + out[rows : 2 * rows] + out[2 * rows :]


NN_DIMS = ((1,), (0,))
NT_DIMS = ((1,), (1,))


def kernel(
    ny, nz, nf,
    flow, visc, jac, rbf, cols, owner, kmat, kcols,
    out_flow, out_shell, out_motion,
    raw, left, right, q0, q1, q2, rbf_v, kw,
    pick, pack, nodes_out, nodes_in, one_hot, one_hot_t, loads_out, loads_in, lhs,
    part_out, part_in, force_out, force_in, dots1_a, dots1_b, dots2_a, dots2_b,
    ans_out, ans_in, vals_out, vals_in, ssem, rsem, lsem,
):
    nc = CORES
    ng = ny * nc
    nb = ny * nz * nc
    cap = 128 // nz
    b = lax.axis_index("blk")
    f = lax.axis_index("face")
    y = b // (nz * nc)
    z = (b // nc) % nz
    c = b % nc
    g = y * nc + c

    def near(ob, of):
        return ((b + ob + nb) % nb, (f + of + nf) % nf)

    def along_g(d):
        other = (g + d + ng) % ng
        return ((other // nc) * (nz * nc) + z * nc + other % nc, f)

    def along_z(d):
        return (y * (nz * nc) + ((z + d + nz) % nz) * nc + c, f)

    used = [0]

    def send(src, dst, to):
        i = used[0]
        used[0] += 1
        copy = pltpu.make_async_remote_copy(
            src_ref=src, dst_ref=dst, send_sem=ssem.at[i], recv_sem=rsem.at[i],
            device_id=to, device_id_type=MESH,
        )
        copy.start()
        sent.append(copy)
        return copy

    sent = []

    local_wall = [
        pltpu.make_async_copy(flow.at[:, 0:WALL], raw.at[0:6, 0:WALL, 2:6, :], lsem.at[0]),
        pltpu.make_async_copy(visc.at[0:WALL], raw.at[6, 0:WALL, 2:6, :], lsem.at[1]),
    ]
    nk = visc.shape[0]
    local_rest = [
        pltpu.make_async_copy(flow.at[:, WALL:nk], raw.at[0:6, WALL:nk, 2:6, :], lsem.at[2]),
        pltpu.make_async_copy(visc.at[WALL:nk], raw.at[6, WALL:nk, 2:6, :], lsem.at[3]),
    ]
    local_k = pltpu.make_async_copy(kmat, kw.at[REACH], lsem.at[4])
    local_rbf = pltpu.make_async_copy(rbf, rbf_v, lsem.at[5])
    for copy in local_wall:
        copy.start()
    local_rbf.start()
    for copy in local_rest:
        copy.start()
    local_k.start()

    around = [(ob, of) for of in range(nf) for ob in range(-REACH, REACH + 1) if (ob, of) != (0, 0)]
    peers = [near(ob, of) for ob, of in around]
    peers += [along_g(d) for d in range(1, ng)]
    peers += [along_z(d) for d in range(1, nz)]
    barrier = pltpu.get_barrier_semaphore()
    for peer in peers:
        pl.semaphore_signal(barrier, inc=1, device_id=peer, device_id_type=MESH)

    pick[...] = (iota((1024, 128), 1) == (iota((1024, 128), 0) // 256) * 32 + (iota((1024, 128), 0) % 256) // 8).astype(BF16)
    own = owner[...]
    members = (own == iota((128, nb if nb > 128 else 128), 1)).astype(F32)
    earlier = (iota((128, 128), 0) > iota((128, 128), 1)).astype(F32)
    ahead = jnp.dot(earlier.astype(BF16), members.astype(BF16), preferred_element_type=F32)
    rank = jnp.sum(ahead * members, axis=1, keepdims=True).astype(jnp.int32)
    own_c = own % nc
    own_z = (own // nc) % nz
    own_g = (own // (nz * nc)) * nc + own_c
    slot = own_z * cap + rank
    lane = iota((128, 128), 1)
    for d in range(ng):
        here = (own_g == (g + d) % ng) & (slot == lane)
        pack[:, d * 128 : (d + 1) * 128] = here.astype(F32).astype(BF16)
    named = (cols[...] + 1).astype(F32)
    named = jnp.concatenate([named, jnp.zeros((4, 128), F32)], axis=0)
    packed_nodes = lax.dot_general(
        named.astype(BF16), pack[...], (NN_DIMS, ((), ())), preferred_element_type=F32
    )
    for d in range(ng):
        nodes_out[d] = packed_nodes[:, d * 128 : (d + 1) * 128]

    pl.semaphore_wait(barrier, len(peers))
    for copy in local_wall:
        copy.wait()

    def halo(lo, hi):
        ks = pl.ds(lo, hi - lo)
        low, high = pl.ds(0, 128), pl.ds(128, 128)
        return [
            send(raw.at[:, ks, 4:6, :], raw.at[:, ks, 0:2, :], near(1, 0)),
            send(raw.at[:, ks, 2:4, :], raw.at[:, ks, 6:8, :], near(-1, 0)),
            send(raw.at[:, ks, 2:6, high], left.at[:, ks, 2:6, :], near(0, 1)),
            send(raw.at[:, ks, 2:6, low], right.at[:, ks, 2:6, :], near(0, -1)),
            send(raw.at[:, ks, 5:6, high], left.at[:, ks, 1:2, :], near(1, 1)),
            send(raw.at[:, ks, 5:6, low], right.at[:, ks, 1:2, :], near(1, -1)),
            send(raw.at[:, ks, 2:3, high], left.at[:, ks, 6:7, :], near(-1, 1)),
            send(raw.at[:, ks, 2:3, low], right.at[:, ks, 6:7, :], near(-1, -1)),
        ]

    wall_halo = halo(0, WALL)
    node_copies = [send(nodes_out.at[d], nodes_in.at[d], along_g(d)) for d in range(1, ng)]

    row8 = iota((8, 384), 0)
    lane384 = iota((8, 384), 1)
    inside = ((b > 0) | (row8 >= 2)) & ((b < nb - 1) | (row8 < 6))
    inside = inside & ((lane384 < 256) | ((row8 >= 1) & (row8 < 7)))
    inside = inside & ((f < nf - 1) | (lane384 < 256) | (lane384 >= 320))
    inside = inside & ((f > 0) | (lane384 < 320))
    from_right = iota((8, 128), 1) < 64

    zero_plane = jnp.zeros((8, 384), F32)
    for v in range(6):
        for buf in (q0, q1):
            buf[v, 0] = zero_plane
            buf[v, nk + 1] = zero_plane

    def clean(k):
        for v in range(7):
            edge = jnp.where(from_right, right[v, k], left[v, k])
            q0[v, k + 1] = jnp.where(inside, jnp.concatenate([raw[v, k], edge], axis=1), 0.0)

    def relax(src, k, wide, variables):
        diffs = []
        spreads = {}
        centres = {}
        for v in range(6):
            mid = src[v, k + 1]
            trio = [
                (src[v, k + 2, :, 0:wide], src[v, k, :, 0:wide]),
                (pltpu.roll(mid, 7, 0)[:, 0:wide], pltpu.roll(mid, 1, 0)[:, 0:wide]),
                (pltpu.roll(mid, 383, 1)[:, 0:wide], pltpu.roll(mid, 1, 1)[:, 0:wide]),
            ]
            diffs.append([0.5 * (hi - lo) for hi, lo in trio])
            if v in variables:
                centres[v] = mid[:, 0:wide]
                total = -6.0 * centres[v]
                for hi, lo in trio:
                    total = total + hi + lo
                spreads[v] = total
        visc_here = q0[6, k + 1, :, 0:wide]
        result = []
        for i in variables:
            moved = None
            for d in range(3):
                for v in range(6):
                    term = jac[(d * 6 + i) * 6 + v] * diffs[v][d]
                    moved = term if moved is None else moved + term
            result.append(centres[i] - moved + visc_here * spreads[i])
        return result

    def first_sweep(k):
        for v, val in enumerate(relax(q0, k, 384, range(6))):
            q1[v, k + 1] = jnp.where(inside, val, 0.0)

    for copy in wall_halo:
        copy.wait_recv()
    for k in range(WALL):
        clean(k)
    for k in range(WALL - 1):
        first_sweep(k)
    wall = relax(q1, 0, 256, [0])[0]
    of_point = iota((8, 256), 1) % 8 == iota((8, 256), 0)
    spread_wall = jnp.concatenate(
        [jnp.where(of_point, jnp.broadcast_to(wall[2 + i : 3 + i], (8, 256)), 0.0) for i in range(4)],
        axis=1,
    )
    pressure = exact_dot(spread_wall, pick[...], NN_DIMS)
    local_rbf.wait()
    loads = None
    for p in range(8):
        term = rbf_v[p] * pressure[p : p + 1]
        loads = term if loads is None else loads + term
    gap = jnp.zeros((2, 128), F32)
    tall = []
    for k in range(4):
        tall += [loads[k * 6 : k * 6 + 6], gap]
    packed = exact_dot(jnp.concatenate(tall, axis=0), pack[...], NN_DIMS)
    for d in range(ng):
        loads_out[d] = packed[:, d * 128 : (d + 1) * 128]
    load_copies = [send(loads_out.at[d], loads_in.at[d], along_g(d)) for d in range(1, ng)]

    for copy in local_rest:
        copy.wait()
    rest_halo = halo(WALL, nk)
    local_k.wait()
    k_copies = [send(kw.at[REACH], kw.at[REACH - o], near(o, 0)) for o in (1, -1, 2, -2)]

    nodes_in[0] = nodes_out[0]
    loads_in[0] = loads_out[0]
    for copy in node_copies:
        copy.wait_recv()
    lane256 = iota((128, 256), 1) + 1
    for d in range(ng):
        upright = jnp.transpose(
            jnp.concatenate([nodes_in[d], jnp.zeros((120, 128), F32)], axis=0)
        ).astype(jnp.int32)
        for k in range(4):
            hit = upright[:, k : k + 1] == lane256
            one_hot[(d * 4 + k) * 128 : (d * 4 + k + 1) * 128, :] = hit.astype(F32).astype(BF16)

    for copy in load_copies:
        copy.wait_recv()
    slot_z = iota((nz, 24, 128), 2) // cap
    dest_z = (iota((nz, 24, 128), 0) + z) % nz
    to_dest = slot_z == dest_z
    for d in range(ng):
        for k in range(4):
            parts = stacked_parts(loads_in[d, k * 8 : k * 8 + 8, :])
            masked = jnp.where(to_dest, jnp.broadcast_to(parts[None], (nz, 24, 128)), 0.0)
            at = (d * 4 + k) * 128
            lhs[:, at : at + 128] = masked.reshape(nz * 24, 128).astype(BF16)
    dense = jnp.dot(lhs[...], one_hot[...], preferred_element_type=F32)
    for d in range(nz):
        part = dense[d * 24 : d * 24 + 24]
        part_out[d] = part[0:8] + part[8:16] + part[16:24]
    part_copies = [
        send(part_out.at[d, 0:6, :], part_in.at[d, 0:6, :], along_z(d)) for d in range(1, nz)
    ]

    for copy in rest_halo:
        copy.wait_recv()

    def clean_loop(k, carry):
        clean(k)
        return carry

    def first_loop(k, carry):
        first_sweep(k)
        return carry

    lax.fori_loop(WALL, nk, clean_loop, 0)
    lax.fori_loop(WALL - 1, nk, first_loop, 0)

    total = part_out[0, 0:6, :]
    for d in range(1, nz):
        part_copies[d - 1].wait_recv()
        total = total + part_in[d, 0:6, :]
    force_out[...] = total
    force_copies = {}
    for ob, of in around:
        force_copies[ob, of] = send(force_out, force_in.at[of, ob + REACH], near(ob, of))

    for d in range(ng):
        for k in range(4):
            row = nodes_in[d, k : k + 1, :].astype(jnp.int32)
            hit = row == iota((256, 128), 0) + 1
            at = (d * 4 + k) * 128
            one_hot_t[:, at : at + 128] = hit.astype(F32).astype(BF16)

    def second_loop(k, carry):
        for v, val in enumerate(relax(q1, k, 256, range(6))):
            q2[v, k] = val
        return carry

    lax.fori_loop(0, nk, second_loop, 0)
    flow_copy = pltpu.make_async_copy(q2.at[:, :, 2:6, :], out_flow, lsem.at[6])
    flow_copy.start()

    for copy in force_copies.values():
        copy.wait_recv()
    for copy in k_copies:
        copy.wait_recv()

    def of_face(ob, df):
        return force_out[...] if (ob, df) == (0, 0) else force_in[df, ob + REACH]

    valid = [(b + p >= 0) & (b + p < nb) for p in range(-REACH, REACH + 1)]
    empty = jnp.zeros((2, 128), F32)
    start = []
    for p in range(-REACH, REACH + 1):
        terms = [of_face(-p, df) for df in range(nf)]
        if nf == 4:
            full = (terms[0] + terms[2]) + (terms[1] + terms[3])
        else:
            full = terms[0] + terms[1]
        full = jnp.where(valid[p + REACH], full, 0.0)
        for half in range(2):
            start.append(jnp.concatenate([full[:, half * 128 : half * 128 + 128], empty], axis=0))
    v0 = dict(enumerate(start))

    reach = [kcols[j, 0] for j in range(8)]
    lane128 = iota((8, 128), 1)

    def times_k(vec, lo, hi):
        shifted = {i: [vec[i]] for i in range(lo, hi)}
        for j in range(1, 7):
            rest = reach[j] % 128
            whole = reach[j] // 128
            back = (128 - rest) % 128
            turned = {i: pltpu.roll(vec[i], back, 1) for i in range(lo - 1, hi + 1)}
            stay = lane128 + rest < 128
            joined = {i: jnp.where(stay, turned[i], turned[i + 1]) for i in range(lo - 1, hi)}
            for i in range(lo, hi):
                far = jnp.where(whole == 1, joined[i], turned[i + 1])
                shifted[i].append(jnp.where(whole == 0, joined[i - 1], far))
        for i in range(lo, hi):
            shifted[i].append(vec[i])
        out = {}
        for i in range(lo, hi):
            lanes = pl.ds((i % 2) * 128, 128)
            rows = []
            for r in range(DOF):
                total = None
                for j in range(8):
                    term = kw[i // 2, j, r, :, lanes] * shifted[i][j][0:6]
                    total = term if total is None else total + term
                rows.append(jnp.sum(total, axis=0, keepdims=True))
            rows.append(empty)
            out[i] = jnp.where(valid[i // 2], jnp.concatenate(rows, axis=0), 0.0)
        return out

    mid = (2 * REACH, 2 * REACH + 1)

    def dot_row(one, two):
        return jnp.sum(sum(one[i] * two[i] for i in mid), axis=0, keepdims=True)

    def everywhere(rows, buf_a, buf_b):
        height = buf_a.shape[1]
        rows = rows + [jnp.zeros((height - len(rows), 128), F32)]
        buf_a[0] = jnp.concatenate(rows, axis=0)
        copies = [send(buf_a.at[0], buf_a.at[d], along_z(d)) for d in range(1, nz)]
        for copy in copies:
            copy.wait_recv()
        buf_b[0] = functools.reduce(jnp.add, [buf_a[d] for d in range(nz)])
        copies = [send(buf_b.at[0], buf_b.at[d], along_g(d)) for d in range(1, ng)]
        for copy in copies:
            copy.wait_recv()
        total = functools.reduce(jnp.add, [buf_b[d] for d in range(ng)])
        total = jnp.sum(total, axis=1, keepdims=True)
        return [total[i : i + 1] for i in range(len(rows) - 1)]

    def mix(scales_and_vecs, lo, hi):
        out = {}
        for i in range(lo, hi):
            total = None
            for scale, vec in scales_and_vecs:
                term = vec[i] if scale is None else scale * vec[i]
                total = term if total is None else total + term
            out[i] = total
        return out

    v1 = times_k(v0, 1, 9)
    v2 = times_k(v1, 2, 8)
    m0, m1, m2, m3 = everywhere(
        [dot_row(v0, v0), dot_row(v0, v1), dot_row(v1, v1), dot_row(v1, v2)], dots1_a, dots1_b
    )
    alpha0 = m0 / m1
    rr1 = jnp.maximum(m0 - 2.0 * alpha0 * m1 + alpha0 * alpha0 * m2, 0.0)
    beta0 = rr1 / m0
    bend1 = (m1 - 2.0 * alpha0 * m2 + alpha0 * alpha0 * m3) + 2.0 * beta0 * (m1 - alpha0 * m2) + beta0 * beta0 * m1
    alpha1 = rr1 / bend1
    r1 = mix([(None, v0), (-alpha0, v1)], 2, 8)
    d1 = mix([(None, r1), (beta0, v0)], 2, 8)
    t = mix([(1.0 + beta0, v1), (-alpha0, v2)], 2, 8)
    x2 = mix([(alpha0, v0), (alpha1, d1)], 4, 6)
    r2 = mix([(None, r1), (-alpha1, t)], 2, 8)
    s = times_k(r2, 3, 7)
    u = times_k(s, 4, 6)
    w = times_k(t, 4, 6)
    pairs = [(r2, r2), (r2, s), (r2, t), (d1, t), (s, s), (s, t), (t, t), (s, u), (s, w), (t, w)]
    rr2, rs, rt, dt, ss, st, tt, su, sw, tw = everywhere(
        [dot_row(one, two) for one, two in pairs], dots2_a, dots2_b
    )
    beta1 = rr2 / rr1
    bend2 = rs + 2.0 * beta1 * rt + beta1 * beta1 * dt
    alpha2 = rr2 / bend2
    along = rs + beta1 * rt
    square = ss + 2.0 * beta1 * st + beta1 * beta1 * tt
    rr3 = jnp.maximum(rr2 - 2.0 * alpha2 * along + alpha2 * alpha2 * square, 0.0)
    beta2 = rr3 / rr2
    bend3 = (
        rs
        - 2.0 * alpha2 * (ss + beta1 * st)
        + alpha2 * alpha2 * (su + 2.0 * beta1 * sw + beta1 * beta1 * tw)
        + 2.0 * beta2 * (along - alpha2 * square)
        + beta2 * beta2 * bend2
    )
    alpha3 = rr3 / bend3
    d2 = mix([(None, r2), (beta1, d1)], 4, 6)
    w2 = mix([(None, s), (beta1, t)], 4, 6)
    r3 = mix([(None, r2), (-alpha2, w2)], 4, 6)
    d3 = mix([(None, r3), (beta2, d2)], 4, 6)
    x4 = mix([(None, x2), (alpha2, d2), (alpha3, d3)], 4, 6)
    answer = jnp.concatenate([x4[4], x4[5]], axis=1)
    ans_out[...] = answer
    ans_copies = [
        send(ans_out.at[0:6, :], ans_in.at[d, 0:6, :], along_z(d)) for d in range(1, nz)
    ]
    out_shell[...] = answer[0:6]

    level = []
    zero2 = jnp.zeros((2, 256), F32)
    for d in range(nz):
        if d == 0:
            level.append(stacked_parts(answer))
        else:
            ans_copies[d - 1].wait_recv()
            level.append(stacked_parts(jnp.concatenate([ans_in[d, 0:6, :], zero2], axis=0)))
    wide_x = jnp.concatenate(level, axis=0).astype(BF16)
    from_z = (z + nz - iota((nz, 8, 256), 0)) % nz
    from_here = (iota((nz, 8, 256), 2) % 128) // cap == from_z
    for d in range(ng):
        for k in (0, 2):
            at = (d * 4 + k) * 128
            got = jnp.dot(wide_x, one_hot_t[:, at : at + 256], preferred_element_type=F32)
            got = got.reshape(nz, 3, 8, 256)
            got = got[:, 0] + got[:, 1] + got[:, 2]
            got = jnp.sum(jnp.where(from_here, got, 0.0), axis=0)
            vals_out[d, k * 8 : k * 8 + 8, :] = got[:, 0:128]
            vals_out[d, k * 8 + 8 : k * 8 + 16, :] = got[:, 128:256]
    val_copies = [send(vals_out.at[d], vals_in.at[d], along_g(-d)) for d in range(1, ng)]
    returned = [vals_out[0]]
    for d in range(1, ng):
        val_copies[d - 1].wait_recv()
        returned.append(vals_in[d])
    values = exact_dot(jnp.concatenate(returned, axis=1), pack[...], NT_DIMS)
    values = jnp.concatenate([values[k * 8 : k * 8 + 6] for k in range(4)], axis=0)
    motion = [jnp.sum(rbf_v[p] * values, axis=0, keepdims=True) for p in range(8)]
    out_motion[...] = jnp.concatenate(motion, axis=0)

    flow_copy.wait()
    for copy in sent:
        copy.wait_send()


def solution(mesh):
    nb, nf = mesh.shape["blk"], mesh.shape["face"]
    ny = 4 if nb == 128 else 2
    nz = nb // (ny * CORES)
    ng = ny * CORES
    count = 8 * 2 + 4 + (ng - 1) * 5 + (nz - 1) * 4 + (5 * nf - 1)

    def local(flow, visc, jac, rbf, cols, owner, kmat, kcols):
        nk = visc.shape[0]
        vmem = pl.BlockSpec(memory_space=pltpu.VMEM)
        smem = pl.BlockSpec(memory_space=pltpu.SMEM)
        hbm = pl.BlockSpec(memory_space=pl.ANY)
        k_total = ng * 512
        scratch = [
            ((7, nk, 8, 256), F32),
            ((7, nk, 8, 128), F32),
            ((7, nk, 8, 128), F32),
            ((7, nk + 2, 8, 384), F32),
            ((6, nk + 2, 8, 384), F32),
            ((6, nk, 8, 256), F32),
            ((8, 24, 128), F32),
            ((5, 8, 6, 6, 256), F32),
            ((1024, 128), BF16),
            ((128, ng * 128), BF16),
            ((ng, 8, 128), F32),
            ((ng, 8, 128), F32),
            ((k_total, 256), BF16),
            ((256, k_total), BF16),
            ((ng, 32, 128), F32),
            ((ng, 32, 128), F32),
            ((nz * 24, k_total), BF16),
            ((nz, 8, 256), F32),
            ((nz, 8, 256), F32),
            ((6, 256), F32),
            ((nf, 5, 6, 256), F32),
            ((nz, 8, 128), F32),
            ((ng, 8, 128), F32),
            ((nz, 16, 128), F32),
            ((ng, 16, 128), F32),
            ((8, 256), F32),
            ((nz, 8, 256), F32),
            ((ng, 32, 128), F32),
            ((ng, 32, 128), F32),
        ]
        return pl.pallas_call(
            functools.partial(kernel, ny, nz, nf),
            out_shape=(
                jax.ShapeDtypeStruct(flow.shape, F32),
                jax.ShapeDtypeStruct((6, 256), F32),
                jax.ShapeDtypeStruct((8, 128), F32),
            ),
            in_specs=[hbm, hbm, smem, hbm, vmem, vmem, hbm, smem],
            out_specs=(hbm, vmem, vmem),
            scratch_shapes=[pltpu.VMEM(shape, kind) for shape, kind in scratch]
            + [
                pltpu.SemaphoreType.DMA((count,)),
                pltpu.SemaphoreType.DMA((count,)),
                pltpu.SemaphoreType.DMA((8,)),
            ],
            compiler_params=pltpu.CompilerParams(
                collective_id=0, has_side_effects=True, vmem_limit_bytes=48 * 1024 * 1024
            ),
        )(flow, visc, jac.reshape(-1), rbf, cols, owner, kmat, kcols)

    placed = (
        P(None, None, "blk", "face"),
        P(None, "blk", "face"),
        P(),
        P(None, None, ("blk", "face")),
        P(None, ("blk", "face")),
        P(("blk", "face"), None),
        P(None, None, None, "blk"),
        P(None, "blk"),
    )
    return jax.shard_map(
        local,
        mesh=mesh,
        in_specs=placed,
        out_specs=(P(None, None, "blk", "face"), P(None, "blk"), P(None, ("blk", "face"))),
        check_vma=False,
    )
```

```python
import functools

import jax
import jax.numpy as jnp
from jax import lax
from jax.experimental import pallas as pl
from jax.experimental.pallas import tpu as pltpu
from jax.sharding import PartitionSpec as P

MESH = pl.DeviceIdType.MESH
F32 = jnp.float32
BF16 = jnp.bfloat16
DOF = 6
WALL = 3
CORES = 2
CG_ITERS = 4
REACH = 2


def iota(shape, dim):
    return lax.broadcasted_iota(jnp.int32, shape, dim)


def three_parts(x):
    high = x.astype(BF16).astype(F32)
    rest = x - high
    middle = rest.astype(BF16).astype(F32)
    return high, middle, rest - middle


def stacked_parts(x):
    return jnp.concatenate(three_parts(x), axis=0)


def exact_dot(x, table, dims):
    rows = x.shape[0]
    out = lax.dot_general(
        stacked_parts(x).astype(BF16), table, (dims, ((), ())), preferred_element_type=F32
    )
    return out[:rows] + out[rows : 2 * rows] + out[2 * rows :]


def split(x):
    big = 4097.0 * x
    high = big - (big - x)
    return high, x - high


def times_exact(one, two, one_parts, two_parts):
    (one_h, one_l), (two_h, two_l) = one_parts, two_parts
    high = one * two
    low = ((one_h * two_h - high) + one_h * two_l + one_l * two_h) + one_l * two_l
    return high, low


def add_pairs(one, two):
    total = one[0] + two[0]
    back = total - one[0]
    error = (one[0] - (total - back)) + (two[0] - back)
    return total, one[1] + two[1] + error


def tree(items):
    while len(items) > 1:
        half = len(items) // 2
        items = [add_pairs(items[i], items[i + half]) for i in range(half)]
    return items[0]


NN_DIMS = ((1,), (0,))
NT_DIMS = ((1,), (1,))


def kernel(
    ny, nz, nf,
    flow, visc, jac, rbf, cols, owner, kmat, kcols,
    out_flow, out_shell, out_motion,
    raw, left, right, q0, q1, q2, rbf_v, kw,
    pick, pack, nodes_out, nodes_in, one_hot, one_hot_t, loads_out, loads_in, lhs,
    part_out, part_in, force_out, force_in, dots_a, dots_b,
    ans_out, ans_in, vals_out, vals_in, turn, ssem, rsem, lsem, far_sem,
):
    nc = CORES
    ng = ny * nc
    nb = ny * nz * nc
    cap = 128 // nz
    bits_c, bits_z, bits_cap = (n.bit_length() - 1 for n in (nc, nz, cap))
    b = lax.axis_index("blk")
    f = lax.axis_index("face")
    y = b // (nz * nc)
    z = (b // nc) % nz
    c = b % nc
    g = y * nc + c

    def near(ob, of):
        return ((b + ob + nb) % nb, (f + of + nf) % nf)

    def along_g(d):
        other = (g + d + ng) % ng
        return ((other // nc) * (nz * nc) + z * nc + other % nc, f)

    def along_z(d):
        return (y * (nz * nc) + ((z + d + nz) % nz) * nc + c, f)

    used = [0]

    def send(src, dst, to):
        i = used[0]
        used[0] += 1
        copy = pltpu.make_async_remote_copy(
            src_ref=src, dst_ref=dst, send_sem=ssem.at[i], recv_sem=rsem.at[i],
            device_id=to, device_id_type=MESH,
        )
        copy.start()
        sent.append(copy)
        return copy

    sent = []

    local_wall = [
        pltpu.make_async_copy(flow.at[:, 0:WALL], raw.at[0:6, 0:WALL, 2:6, :], lsem.at[0]),
        pltpu.make_async_copy(visc.at[0:WALL], raw.at[6, 0:WALL, 2:6, :], lsem.at[1]),
    ]
    nk = visc.shape[0]
    local_rest = [
        pltpu.make_async_copy(flow.at[:, WALL:nk], raw.at[0:6, WALL:nk, 2:6, :], lsem.at[2]),
        pltpu.make_async_copy(visc.at[WALL:nk], raw.at[6, WALL:nk, 2:6, :], lsem.at[3]),
    ]
    local_k = pltpu.make_async_copy(kmat, kw.at[REACH], lsem.at[4])
    local_rbf = pltpu.make_async_copy(rbf, rbf_v, lsem.at[5])
    for copy in local_wall:
        copy.start()
    local_rbf.start()
    for copy in local_rest:
        copy.start()
    local_k.start()

    first_z = (1, 2, nz - 2, nz - 1) if nz > 5 else range(1, nz)
    around = [(ob, of) for of in range(nf) for ob in range(-REACH, REACH + 1) if (ob, of) != (0, 0)]
    peers = [near(ob, of) for ob, of in around]
    peers += [along_g(d) for d in range(1, ng)]
    peers += [along_z(d) for d in first_z]
    barrier = pltpu.get_barrier_semaphore()
    for peer in peers:
        pl.semaphore_signal(barrier, inc=1, device_id=peer, device_id_type=MESH)

    at_slot = iota((128, 128), 1) - (iota((128, 128), 0) >> 3)
    for i in range(8):
        pick[i * 128 : i * 128 + 128, :] = (at_slot == i * 16).astype(F32).astype(BF16)
    own = jnp.transpose(jnp.broadcast_to(owner[...], (128, 128)))[:, 0:1]
    members = (own == iota((128, nb if nb > 128 else 128), 1)).astype(F32)
    earlier = (iota((128, 128), 0) > iota((128, 128), 1)).astype(F32)
    ahead = jnp.dot(earlier.astype(BF16), members.astype(BF16), preferred_element_type=F32)
    rank = jnp.sum(ahead * members, axis=1, keepdims=True).astype(jnp.int32)
    own_c = own & (nc - 1)
    own_z = (own >> bits_c) & (nz - 1)
    own_g = (own >> (bits_c + bits_z)) * nc + own_c
    slot = own_z * cap + rank
    lane = iota((128, 128), 1)
    for d in range(ng):
        here = (own_g == (g + d) % ng) & (slot == lane)
        pack[:, d * 128 : (d + 1) * 128] = here.astype(F32).astype(BF16)
    named = (cols[...] + 1).astype(F32)
    named = jnp.concatenate([named, jnp.zeros((4, 128), F32)], axis=0)
    packed_nodes = lax.dot_general(
        named.astype(BF16), pack[...], (NN_DIMS, ((), ())), preferred_element_type=F32
    )
    local_k.wait()
    largest = None
    for r in range(DOF):
        size = sum(jnp.sum(jnp.abs(kw[REACH, r, e]), axis=0, keepdims=True) for e in range(DOF))
        largest = size if largest is None else jnp.maximum(largest, size)
    largest = jnp.broadcast_to(jnp.max(largest, axis=1, keepdims=True), (8, 128))
    node_rows = iota((8, 128), 0) < 4
    for d in range(ng):
        nodes_out[d] = jnp.where(node_rows, packed_nodes[:, d * 128 : (d + 1) * 128], largest)

    pl.semaphore_wait(barrier, len(peers))

    def pass_on(step, sem):
        if nz > 2 * step + 1:
            for d in (step, -step):
                pl.semaphore_signal(sem, inc=1, device_id=along_z(d), device_id_type=MESH)

    def heard(step, sem):
        if nz > 2 * step + 1:
            pl.semaphore_wait(sem, 2)

    pass_on(2, far_sem.at[0])
    for copy in local_wall:
        copy.wait()

    def halo(lo, hi):
        ks = pl.ds(lo, hi - lo)
        low, high = pl.ds(0, 128), pl.ds(128, 128)
        return [
            send(raw.at[:, ks, 4:6, :], raw.at[:, ks, 0:2, :], near(1, 0)),
            send(raw.at[:, ks, 2:4, :], raw.at[:, ks, 6:8, :], near(-1, 0)),
            send(raw.at[:, ks, 2:6, high], left.at[:, ks, 2:6, :], near(0, 1)),
            send(raw.at[:, ks, 2:6, low], right.at[:, ks, 2:6, :], near(0, -1)),
            send(raw.at[:, ks, 5:6, high], left.at[:, ks, 1:2, :], near(1, 1)),
            send(raw.at[:, ks, 5:6, low], right.at[:, ks, 1:2, :], near(1, -1)),
            send(raw.at[:, ks, 2:3, high], left.at[:, ks, 6:7, :], near(-1, 1)),
            send(raw.at[:, ks, 2:3, low], right.at[:, ks, 6:7, :], near(-1, -1)),
        ]

    wall_halo = halo(0, WALL)
    node_copies = [send(nodes_out.at[d], nodes_in.at[d], along_g(d)) for d in range(1, ng)]

    row8 = iota((8, 384), 0)
    lane384 = iota((8, 384), 1)
    inside = ((b > 0) | (row8 >= 2)) & ((b < nb - 1) | (row8 < 6))
    inside = inside & ((lane384 < 256) | ((row8 >= 1) & (row8 < 7)))
    inside = inside & ((f < nf - 1) | (lane384 < 256) | (lane384 >= 320))
    inside = inside & ((f > 0) | (lane384 < 320))
    from_right = iota((8, 128), 1) < 64

    zero_plane = jnp.zeros((8, 384), F32)
    for v in range(6):
        for buf in (q0, q1):
            buf[v, 0] = zero_plane
            buf[v, nk + 1] = zero_plane

    def clean(k):
        for v in range(7):
            edge = jnp.where(from_right, right[v, k], left[v, k])
            q0[v, k + 1] = jnp.where(inside, jnp.concatenate([raw[v, k], edge], axis=1), 0.0)

    def relax(src, k, wide, variables):
        diffs = []
        spreads = {}
        centres = {}
        for v in range(6):
            mid = src[v, k + 1]
            trio = [
                (src[v, k + 2, :, 0:wide], src[v, k, :, 0:wide]),
                (pltpu.roll(mid, 7, 0)[:, 0:wide], pltpu.roll(mid, 1, 0)[:, 0:wide]),
                (pltpu.roll(mid, 383, 1)[:, 0:wide], pltpu.roll(mid, 1, 1)[:, 0:wide]),
            ]
            diffs.append([0.5 * (hi - lo) for hi, lo in trio])
            if v in variables:
                centres[v] = mid[:, 0:wide]
                total = -6.0 * centres[v]
                for hi, lo in trio:
                    total = total + hi + lo
                spreads[v] = total
        visc_here = q0[6, k + 1, :, 0:wide]
        result = []
        for i in variables:
            moved = None
            for d in range(3):
                for v in range(6):
                    term = jac[d, i, v] * diffs[v][d]
                    moved = term if moved is None else moved + term
            result.append(centres[i] - moved + visc_here * spreads[i])
        return result

    def first_sweep(k):
        for v, val in enumerate(relax(q0, k, 384, range(6))):
            q1[v, k + 1] = jnp.where(inside, val, 0.0)

    for copy in wall_halo:
        copy.wait_recv()
    heard(2, far_sem.at[0])
    pass_on(4, far_sem.at[1])
    for k in range(WALL):
        clean(k)
    for k in range(WALL - 1):
        first_sweep(k)
    wall = relax(q1, 0, 256, [0])[0]
    of_point = (iota((8, 256), 1) & 7) == iota((8, 256), 0)
    spread_wall = jnp.concatenate(
        [jnp.where(of_point, jnp.broadcast_to(wall[2 + i : 3 + i], (8, 256)), 0.0) for i in range(4)],
        axis=1,
    )
    pressure = exact_dot(spread_wall, pick[...], NN_DIMS)
    local_rbf.wait()
    loads = None
    for p in range(8):
        term = rbf_v[p] * pressure[p : p + 1]
        loads = term if loads is None else loads + term
    gap = jnp.zeros((2, 128), F32)
    tall = []
    for k in range(4):
        tall += [loads[k * 6 : k * 6 + 6], gap]
    packed = exact_dot(jnp.concatenate(tall, axis=0), pack[...], NN_DIMS)
    for d in range(ng):
        loads_out[d] = packed[:, d * 128 : (d + 1) * 128]
    load_copies = [send(loads_out.at[d], loads_in.at[d], along_g(d)) for d in range(1, ng)]

    nodes_in[0] = nodes_out[0]
    loads_in[0] = loads_out[0]
    for copy in node_copies:
        copy.wait_recv()
    lane256 = iota((128, 256), 1) + 1
    for d in range(ng):
        upright = jnp.transpose(
            jnp.concatenate([nodes_in[d], jnp.zeros((120, 128), F32)], axis=0)
        ).astype(jnp.int32)
        for k in range(4):
            hit = upright[:, k : k + 1] == lane256
            one_hot[(d * 4 + k) * 128 : (d * 4 + k + 1) * 128, :] = hit.astype(F32).astype(BF16)

    for copy in load_copies:
        copy.wait_recv()
    slot_z = iota((nz, 24, 128), 2) >> bits_cap
    dest_z = (iota((nz, 24, 128), 0) + z) & (nz - 1)
    to_dest = slot_z == dest_z
    for d in range(ng):
        for k in range(4):
            parts = stacked_parts(loads_in[d, k * 8 : k * 8 + 8, :])
            masked = jnp.where(to_dest, jnp.broadcast_to(parts[None], (nz, 24, 128)), 0.0)
            at = (d * 4 + k) * 128
            lhs[:, at : at + 128] = masked.reshape(nz * 24, 128).astype(BF16)
    heard(4, far_sem.at[1])
    dense = jnp.dot(lhs[...], one_hot[...], preferred_element_type=F32)
    largest = functools.reduce(jnp.maximum, [nodes_in[d, 4:5, :] for d in range(ng)])
    largest = jnp.concatenate([largest, largest], axis=1)
    for d in range(nz):
        part_out[d, 6:7, :] = largest
        part = dense[d * 24 : d * 24 + 24]
        part_out[d, 0:6, :] = (part[0:8] + part[8:16] + part[16:24])[0:6]
    part_copies = [
        send(part_out.at[d, 0:7, :], part_in.at[d, 0:7, :], along_z(d)) for d in range(1, nz)
    ]

    for copy in local_rest:
        copy.wait()
    rest_halo = halo(WALL, nk)
    k_copies = [send(kw.at[REACH], kw.at[REACH - o], near(o, 0)) for o in (1, -1, 2, -2)]

    for copy in rest_halo:
        copy.wait_recv()

    def clean_loop(k, carry):
        clean(k)
        return carry

    def first_loop(k, carry):
        first_sweep(k)
        return carry

    lax.fori_loop(WALL, nk, clean_loop, 0)
    lax.fori_loop(WALL - 1, nk, first_loop, 0)

    total = part_out[0, 0:6, :]
    for d in range(1, nz):
        part_copies[d - 1].wait_recv()
        total = total + part_in[d, 0:6, :]
        largest = jnp.maximum(largest, part_in[d, 6:7, :])
    scale = 1.0 / largest[:, 0:128]
    force_out[...] = total
    force_copies = {}
    for ob, of in around:
        force_copies[ob, of] = send(force_out, force_in.at[of, ob + REACH], near(ob, of))

    for d in range(ng):
        for k in range(4):
            row = nodes_in[d, k : k + 1, :].astype(jnp.int32)
            hit = row == iota((256, 128), 0) + 1
            at = (d * 4 + k) * 128
            one_hot_t[:, at : at + 128] = hit.astype(F32).astype(BF16)

    def second_loop(k, carry):
        for v, val in enumerate(relax(q1, k, 256, range(6))):
            q2[v, k] = val
        return carry

    lax.fori_loop(0, nk, second_loop, 0)
    flow_copy = pltpu.make_async_copy(q2.at[:, :, 2:6, :], out_flow, lsem.at[6])
    flow_copy.start()

    for copy in force_copies.values():
        copy.wait_recv()
    for copy in k_copies:
        copy.wait_recv()

    def of_face(ob, df):
        return force_out[...] if (ob, df) == (0, 0) else force_in[df, ob + REACH]

    valid = [(b + p >= 0) & (b + p < nb) for p in range(-REACH, REACH + 1)]
    empty = jnp.zeros((2, 128), F32)
    start = []
    for p in range(-REACH, REACH + 1):
        terms = [of_face(-p, df) for df in range(nf)]
        if nf == 4:
            full = (terms[0] + terms[2]) + (terms[1] + terms[3])
        else:
            full = terms[0] + terms[1]
        full = jnp.where(valid[p + REACH], full, 0.0)
        for half in range(2):
            start.append(jnp.concatenate([full[:, half * 128 : half * 128 + 128], empty], axis=0))
    v0 = dict(enumerate(start))

    reach = [kcols[j, 0] for j in range(8)]
    lane128 = iota((8, 128), 1)

    def times_k(vec, lo, hi):
        shifted = {i: [vec[i]] for i in range(lo, hi)}
        for j in range(1, 7):
            rest = reach[j] % 128
            whole = reach[j] // 128
            back = (128 - rest) % 128
            turned = {i: pltpu.roll(vec[i], back, 1) for i in range(lo - 1, hi + 1)}
            stay = lane128 + rest < 128
            joined = {i: jnp.where(stay, turned[i], turned[i + 1]) for i in range(lo - 1, hi)}
            for i in range(lo, hi):
                far = jnp.where(whole == 1, joined[i], turned[i + 1])
                shifted[i].append(jnp.where(whole == 0, joined[i - 1], far))
        for i in range(lo, hi):
            shifted[i].append(vec[i])
            for j in range(8):
                turn[i, j] = shifted[i][j]
        out = {}
        for i in range(lo, hi):
            lanes = pl.ds((i % 2) * 128, 128)
            columns = [turn[i, :, e, :] for e in range(DOF)]
            rows = []
            for r in range(DOF):
                total = None
                for e in range(DOF):
                    term = kw[i // 2, r, e, :, lanes] * columns[e]
                    total = term if total is None else total + term
                rows.append(jnp.sum(total, axis=0, keepdims=True))
            rows.append(empty)
            out[i] = jnp.where(valid[i // 2], jnp.concatenate(rows, axis=0), 0.0)
        return out

    mid = (2 * REACH, 2 * REACH + 1)

    basis = [v0]
    for n in range(CG_ITERS):
        image = times_k(basis[-1], n + 1, 9 - n)
        fresh = {}
        for i in image:
            turned = 2.0 * (scale * image[i]) - basis[-1][i]
            fresh[i] = turned if n == 0 else 2.0 * turned - basis[-2][i]
        basis.append(fresh)

    row_id, lane_id = iota((8, 128), 0), iota((8, 128), 1)
    pairs = [(i, j) for j in range(CG_ITERS + 1) for i in range(min(j + 1, CG_ITERS))]
    halves = [{i: split(vec[i]) for i in mid} for vec in basis]
    tiles = [(jnp.zeros((8, 128), F32), jnp.zeros((8, 128), F32)) for _ in range(2)]
    for at, (m, n) in enumerate(pairs):
        one, two = [times_exact(basis[m][i], basis[n][i], halves[m][i], halves[n][i]) for i in mid]
        both = add_pairs(one, two)
        for step in (4, 2, 1):
            both = add_pairs(both, (pltpu.roll(both[0], step, 0), pltpu.roll(both[1], step, 0)))
        here = row_id == at % 8
        high, low = tiles[at // 8]
        tiles[at // 8] = (jnp.where(here, both[0], high), jnp.where(here, both[1], low))
    for step in (64, 32, 16, 8, 4, 2, 1):
        tiles = [add_pairs(t, (pltpu.roll(t[0], step, 1), pltpu.roll(t[1], step, 1))) for t in tiles]
    for part in range(2):
        line = sum(
            jnp.sum(jnp.where(lane_id == row_id + 8 * k, tiles[k][part], 0.0), axis=0, keepdims=True)
            for k in range(2)
        )
        dots_a[0, part : part + 1, :] = line
    copies = [send(dots_a.at[0], dots_a.at[d], along_z(d)) for d in range(1, nz)]
    for copy in copies:
        copy.wait_recv()
    line = tree([(dots_a[d, 0:1, :], dots_a[d, 1:2, :]) for d in range(nz)])
    for part in range(2):
        dots_b[0, part : part + 1, :] = line[part]
    copies = [send(dots_b.at[0], dots_b.at[d], along_g(d)) for d in range(1, ng)]
    for copy in copies:
        copy.wait_recv()
    line = tree([(dots_b[d, 0:1, :], dots_b[d, 1:2, :]) for d in range(ng)])
    gram = []
    for j in range(CG_ITERS):
        spots = None
        for i in range(CG_ITERS + 1):
            at = pairs.index((min(i, j), max(i, j)))
            spot = (row_id == i) & (lane_id == at)
            spots = spot if spots is None else spots | spot
        column = []
        for part in line:
            picked = jnp.where(spots, jnp.broadcast_to(part, (8, 128)), 0.0)
            column.append(jnp.broadcast_to(jnp.sum(picked, axis=1, keepdims=True), (8, 128)))
        gram.append((column[0], column[1], split(column[0])))

    def entry(vec, j):
        return jnp.broadcast_to(vec[j : j + 1], (8, 128))

    def times_gram(vec, terms):
        total = None
        for j in range(terms):
            by = entry(vec, j)
            high, low = times_exact(gram[j][0], by, gram[j][2], split(by))
            term = (high, low + gram[j][1] * by)
            total = term if total is None else add_pairs(total, term)
        return total[0] + total[1]

    def inner(one, two):
        return jnp.broadcast_to(jnp.sum(one * two, axis=0, keepdims=True), (8, 128))

    def ratio(top, bottom):
        return jnp.where(bottom > 0.0, top / bottom, 0.0)

    def mapped(vec):
        below = pltpu.roll(vec, 1, 0)
        below = jnp.where(row_id == 1, 2.0 * below, below)
        return jnp.where(row_id < 7, 0.5 * vec + 0.25 * (below + pltpu.roll(vec, 7, 0)), 0.0)

    resid = jnp.where(row_id == 0, 1.0, 0.0)
    course = resid
    weights = jnp.zeros((8, 128), F32)
    norm = inner(resid, times_gram(resid, 1))
    for n in range(CG_ITERS):
        moved = mapped(course)
        alpha = ratio(norm, inner(moved, times_gram(course, n + 1)))
        weights = weights + alpha * course
        if n < CG_ITERS - 1:
            resid = resid - alpha * moved
            fresh_norm = jnp.maximum(inner(resid, times_gram(resid, n + 2)), 0.0)
            course = resid + ratio(fresh_norm, norm) * course
            norm = fresh_norm
    answer = []
    for i in mid:
        total = None
        for n in range(CG_ITERS):
            term = entry(weights, n) * basis[n][i]
            total = term if total is None else total + term
        answer.append(scale * total)
    answer = jnp.concatenate(answer, axis=1)
    ans_out[...] = answer
    ans_copies = [
        send(ans_out.at[0:6, :], ans_in.at[d, 0:6, :], along_z(d)) for d in range(1, nz)
    ]
    out_shell[...] = answer[0:6]

    level = []
    zero2 = jnp.zeros((2, 256), F32)
    for d in range(nz):
        if d == 0:
            level.append(stacked_parts(answer))
        else:
            ans_copies[d - 1].wait_recv()
            level.append(stacked_parts(jnp.concatenate([ans_in[d, 0:6, :], zero2], axis=0)))
    wide_x = jnp.concatenate(level, axis=0).astype(BF16)
    from_z = (z + nz - iota((nz, 8, 256), 0)) & (nz - 1)
    from_here = (iota((nz, 8, 256), 2) & 127) >> bits_cap == from_z
    for d in range(ng):
        for k in (0, 2):
            at = (d * 4 + k) * 128
            got = jnp.dot(wide_x, one_hot_t[:, at : at + 256], preferred_element_type=F32)
            got = got.reshape(nz, 3, 8, 256)
            got = got[:, 0] + got[:, 1] + got[:, 2]
            got = jnp.sum(jnp.where(from_here, got, 0.0), axis=0)
            vals_out[d, k * 8 : k * 8 + 8, :] = got[:, 0:128]
            vals_out[d, k * 8 + 8 : k * 8 + 16, :] = got[:, 128:256]
    val_copies = [send(vals_out.at[d], vals_in.at[d], along_g(-d)) for d in range(1, ng)]
    returned = [vals_out[0]]
    for d in range(1, ng):
        val_copies[d - 1].wait_recv()
        returned.append(vals_in[d])
    values = exact_dot(jnp.concatenate(returned, axis=1), pack[...], NT_DIMS)
    values = jnp.concatenate([values[k * 8 : k * 8 + 6] for k in range(4)], axis=0)
    motion = [jnp.sum(rbf_v[p] * values, axis=0, keepdims=True) for p in range(8)]
    out_motion[...] = jnp.concatenate(motion, axis=0)

    flow_copy.wait()
    for copy in sent:
        copy.wait_send()


def solution(mesh):
    nb, nf = mesh.shape["blk"], mesh.shape["face"]
    ny = 4 if nb == 128 else 2
    nz = nb // (ny * CORES)
    ng = ny * CORES
    count = 8 * 2 + 4 + (ng - 1) * 4 + (nz - 1) * 3 + (5 * nf - 1)

    def local(flow, visc, jac, rbf, cols, owner, kmat, kcols):
        nk = visc.shape[0]
        vmem = pl.BlockSpec(memory_space=pltpu.VMEM)
        smem = pl.BlockSpec(memory_space=pltpu.SMEM)
        hbm = pl.BlockSpec(memory_space=pl.ANY)
        k_total = ng * 512
        scratch = [
            ((7, nk, 8, 256), F32),
            ((7, nk, 8, 128), F32),
            ((7, nk, 8, 128), F32),
            ((7, nk + 2, 8, 384), F32),
            ((6, nk + 2, 8, 384), F32),
            ((6, nk, 8, 256), F32),
            ((8, 24, 128), F32),
            ((5, 6, 6, 8, 256), F32),
            ((1024, 128), BF16),
            ((128, ng * 128), BF16),
            ((ng, 8, 128), F32),
            ((ng, 8, 128), F32),
            ((k_total, 256), BF16),
            ((256, k_total), BF16),
            ((ng, 32, 128), F32),
            ((ng, 32, 128), F32),
            ((nz * 24, k_total), BF16),
            ((nz, 8, 256), F32),
            ((nz, 8, 256), F32),
            ((6, 256), F32),
            ((nf, 5, 6, 256), F32),
            ((nz, 2, 128), F32),
            ((ng, 2, 128), F32),
            ((8, 256), F32),
            ((nz, 8, 256), F32),
            ((ng, 32, 128), F32),
            ((ng, 32, 128), F32),
            ((10, 8, 8, 128), F32),
        ]
        return pl.pallas_call(
            functools.partial(kernel, ny, nz, nf),
            out_shape=(
                jax.ShapeDtypeStruct(flow.shape, F32),
                jax.ShapeDtypeStruct((6, 256), F32),
                jax.ShapeDtypeStruct((8, 128), F32),
            ),
            in_specs=[hbm, hbm, smem, hbm, vmem, vmem, hbm, smem],
            out_specs=(hbm, vmem, vmem),
            scratch_shapes=[pltpu.VMEM(shape, kind) for shape, kind in scratch]
            + [
                pltpu.SemaphoreType.DMA((count,)),
                pltpu.SemaphoreType.DMA((count,)),
                pltpu.SemaphoreType.DMA((8,)),
                pltpu.SemaphoreType.REGULAR((2,)),
            ],
            compiler_params=pltpu.CompilerParams(
                collective_id=0, has_side_effects=True, vmem_limit_bytes=60 * 1024 * 1024
            ),
        )(flow, visc, jac, rbf, cols, owner.reshape(1, -1), kmat.transpose(1, 2, 0, 3), kcols)

    placed = (
        P(None, None, "blk", "face"),
        P(None, "blk", "face"),
        P(),
        P(None, None, ("blk", "face")),
        P(None, ("blk", "face")),
        P(("blk", "face"), None),
        P(None, None, None, "blk"),
        P(None, "blk"),
    )
    return jax.shard_map(
        local,
        mesh=mesh,
        in_specs=placed,
        out_specs=(P(None, None, "blk", "face"), P(None, "blk"), P(None, ("blk", "face"))),
        check_vma=False,
    )
```

```python
import functools

import jax
import jax.numpy as jnp
from jax import lax
from jax.experimental import pallas as pl
from jax.experimental.pallas import tpu as pltpu
from jax.sharding import PartitionSpec as P

MESH = pl.DeviceIdType.MESH
F32 = jnp.float32
BF16 = jnp.bfloat16
DOF = 6
WALL = 3
CORES = 2
CG_ITERS = 4
REACH = 2


def iota(shape, dim):
    return lax.broadcasted_iota(jnp.int32, shape, dim)


def three_parts(x):
    high = x.astype(BF16).astype(F32)
    rest = x - high
    middle = rest.astype(BF16).astype(F32)
    return high, middle, rest - middle


def stacked_parts(x):
    return jnp.concatenate(three_parts(x), axis=0)


def exact_dot(x, table, dims):
    rows = x.shape[0]
    out = lax.dot_general(
        stacked_parts(x).astype(BF16), table, (dims, ((), ())), preferred_element_type=F32
    )
    return out[:rows] + out[rows : 2 * rows] + out[2 * rows :]


def split(x):
    big = 4097.0 * x
    high = big - (big - x)
    return high, x - high


def times_exact(one, two, one_parts, two_parts):
    (one_h, one_l), (two_h, two_l) = one_parts, two_parts
    high = one * two
    low = ((one_h * two_h - high) + one_h * two_l + one_l * two_h) + one_l * two_l
    return high, low


def add_pairs(one, two):
    total = one[0] + two[0]
    back = total - one[0]
    error = (one[0] - (total - back)) + (two[0] - back)
    return total, one[1] + two[1] + error


def tree(items):
    while len(items) > 1:
        half = len(items) // 2
        items = [add_pairs(items[i], items[i + half]) for i in range(half)]
    return items[0]


NN_DIMS = ((1,), (0,))
NT_DIMS = ((1,), (1,))


def kernel(
    ny, nz, nf,
    flow, visc, jac, rbf, cols, owner, kmat, kcols,
    out_flow, out_shell, out_motion,
    raw, left, right, q0, q1, q2, rbf_v, kw,
    pick, pack, nodes_out, nodes_in, one_hot, one_hot_t, loads_out, loads_in, lhs,
    part_out, part_in, force_out, force_in, dots_a, dots_b,
    ans_out, ans_in, vals_out, vals_in, turn, ssem, rsem, lsem, far_sem,
):
    nc = CORES
    ng = ny * nc
    nb = ny * nz * nc
    cap = 128 // nz
    bits_c, bits_z, bits_cap = (n.bit_length() - 1 for n in (nc, nz, cap))
    b = lax.axis_index("blk")
    f = lax.axis_index("face")
    y = b // (nz * nc)
    z = (b // nc) % nz
    c = b % nc
    g = y * nc + c

    def near(ob, of):
        return ((b + ob + nb) % nb, (f + of + nf) % nf)

    def along_g(d):
        other = (g + d + ng) % ng
        return ((other // nc) * (nz * nc) + z * nc + other % nc, f)

    def along_z(d):
        return (y * (nz * nc) + ((z + d + nz) % nz) * nc + c, f)

    used = [0]

    def send(src, dst, to):
        i = used[0]
        used[0] += 1
        copy = pltpu.make_async_remote_copy(
            src_ref=src, dst_ref=dst, send_sem=ssem.at[i], recv_sem=rsem.at[i],
            device_id=to, device_id_type=MESH,
        )
        copy.start()
        sent.append(copy)
        return copy

    sent = []

    local_wall = [
        pltpu.make_async_copy(flow.at[:, 0:WALL], raw.at[0:6, 0:WALL, 2:6, :], lsem.at[0]),
        pltpu.make_async_copy(visc.at[0:WALL], raw.at[6, 0:WALL, 2:6, :], lsem.at[1]),
    ]
    nk = visc.shape[0]
    local_rest = [
        pltpu.make_async_copy(flow.at[:, WALL:nk], raw.at[0:6, WALL:nk, 2:6, :], lsem.at[2]),
        pltpu.make_async_copy(visc.at[WALL:nk], raw.at[6, WALL:nk, 2:6, :], lsem.at[3]),
    ]
    local_k = pltpu.make_async_copy(kmat, kw.at[REACH], lsem.at[4])
    local_rbf = pltpu.make_async_copy(rbf, rbf_v, lsem.at[5])
    for copy in local_wall:
        copy.start()
    local_rbf.start()
    for copy in local_rest:
        copy.start()
    local_k.start()

    first_z = (1, 2, nz - 2, nz - 1) if nz > 5 else range(1, nz)
    around = [(ob, of) for of in range(nf) for ob in range(-REACH, REACH + 1) if (ob, of) != (0, 0)]
    peers = [near(ob, of) for ob, of in around]
    peers += [along_g(d) for d in range(1, ng)]
    peers += [along_z(d) for d in first_z]
    barrier = pltpu.get_barrier_semaphore()
    for peer in peers:
        pl.semaphore_signal(barrier, inc=1, device_id=peer, device_id_type=MESH)

    at_slot = iota((128, 128), 1) - (iota((128, 128), 0) >> 3)
    for i in range(8):
        pick[i * 128 : i * 128 + 128, :] = (at_slot == i * 16).astype(F32).astype(BF16)
    own = jnp.transpose(jnp.broadcast_to(owner[...], (128, 128)))[:, 0:1]
    members = (own == iota((128, nb if nb > 128 else 128), 1)).astype(F32)
    earlier = (iota((128, 128), 0) > iota((128, 128), 1)).astype(F32)
    ahead = jnp.dot(earlier.astype(BF16), members.astype(BF16), preferred_element_type=F32)
    rank = jnp.sum(ahead * members, axis=1, keepdims=True).astype(jnp.int32)
    own_c = own & (nc - 1)
    own_z = (own >> bits_c) & (nz - 1)
    own_g = (own >> (bits_c + bits_z)) * nc + own_c
    slot = own_z * cap + rank
    lane = iota((128, 128), 1)
    for d in range(ng):
        here = (own_g == (g + d) % ng) & (slot == lane)
        pack[:, d * 128 : (d + 1) * 128] = here.astype(F32).astype(BF16)
    named = (cols[...] + 1).astype(F32)
    named = jnp.concatenate([named, jnp.zeros((4, 128), F32)], axis=0)
    packed_nodes = lax.dot_general(
        named.astype(BF16), pack[...], (NN_DIMS, ((), ())), preferred_element_type=F32
    )
    local_k.wait()
    largest = None
    for r in range(DOF):
        size = sum(jnp.sum(jnp.abs(kw[REACH, r, e]), axis=0, keepdims=True) for e in range(DOF))
        largest = size if largest is None else jnp.maximum(largest, size)
    largest = jnp.broadcast_to(jnp.max(largest, axis=1, keepdims=True), (8, 128))
    node_rows = iota((8, 128), 0) < 4
    for d in range(ng):
        nodes_out[d] = jnp.where(node_rows, packed_nodes[:, d * 128 : (d + 1) * 128], largest)

    pl.semaphore_wait(barrier, len(peers))

    def pass_on(step, sem):
        if nz > 2 * step + 1:
            for d in (step, -step):
                pl.semaphore_signal(sem, inc=1, device_id=along_z(d), device_id_type=MESH)

    def heard(step, sem):
        if nz > 2 * step + 1:
            pl.semaphore_wait(sem, 2)

    pass_on(2, far_sem.at[0])
    for copy in local_wall:
        copy.wait()

    def halo(lo, hi):
        ks = pl.ds(lo, hi - lo)
        low, high = pl.ds(0, 128), pl.ds(128, 128)
        return [
            send(raw.at[:, ks, 4:6, :], raw.at[:, ks, 0:2, :], near(1, 0)),
            send(raw.at[:, ks, 2:4, :], raw.at[:, ks, 6:8, :], near(-1, 0)),
            send(raw.at[:, ks, 2:6, high], left.at[:, ks, 2:6, :], near(0, 1)),
            send(raw.at[:, ks, 2:6, low], right.at[:, ks, 2:6, :], near(0, -1)),
            send(raw.at[:, ks, 5:6, high], left.at[:, ks, 1:2, :], near(1, 1)),
            send(raw.at[:, ks, 5:6, low], right.at[:, ks, 1:2, :], near(1, -1)),
            send(raw.at[:, ks, 2:3, high], left.at[:, ks, 6:7, :], near(-1, 1)),
            send(raw.at[:, ks, 2:3, low], right.at[:, ks, 6:7, :], near(-1, -1)),
        ]

    wall_halo = halo(0, WALL)
    node_copies = [send(nodes_out.at[d], nodes_in.at[d], along_g(d)) for d in range(1, ng)]

    k_copies = [send(kw.at[REACH], kw.at[REACH - o], near(o, 0)) for o in (1, -1)]
    for o, half in ((2, pl.ds(128, 128)), (-2, pl.ds(0, 128))):
        k_copies.append(send(kw.at[REACH, :, :, :, half], kw.at[REACH - o, :, :, :, half], near(o, 0)))
    for copy in local_rest:
        copy.wait()

    row8 = iota((8, 384), 0)
    lane384 = iota((8, 384), 1)
    inside = ((b > 0) | (row8 >= 2)) & ((b < nb - 1) | (row8 < 6))
    inside = inside & ((lane384 < 256) | ((row8 >= 1) & (row8 < 7)))
    inside = inside & ((f < nf - 1) | (lane384 < 256) | (lane384 >= 320))
    inside = inside & ((f > 0) | (lane384 < 320))
    from_right = iota((8, 128), 1) < 64

    zero_plane = jnp.zeros((8, 384), F32)
    for v in range(6):
        for buf in (q0, q1):
            buf[v, 0] = zero_plane
            buf[v, nk + 1] = zero_plane

    def clean(k):
        for v in range(7):
            edge = jnp.where(from_right, right[v, k], left[v, k])
            q0[v, k + 1] = jnp.where(inside, jnp.concatenate([raw[v, k], edge], axis=1), 0.0)

    def relax(src, k, wide, variables):
        diffs = []
        spreads = {}
        centres = {}
        for v in range(6):
            mid = src[v, k + 1]
            trio = [
                (src[v, k + 2, :, 0:wide], src[v, k, :, 0:wide]),
                (pltpu.roll(mid, 7, 0)[:, 0:wide], pltpu.roll(mid, 1, 0)[:, 0:wide]),
                (pltpu.roll(mid, 383, 1)[:, 0:wide], pltpu.roll(mid, 1, 1)[:, 0:wide]),
            ]
            diffs.append([0.5 * (hi - lo) for hi, lo in trio])
            if v in variables:
                centres[v] = mid[:, 0:wide]
                total = -6.0 * centres[v]
                for hi, lo in trio:
                    total = total + hi + lo
                spreads[v] = total
        visc_here = q0[6, k + 1, :, 0:wide]
        result = []
        for i in variables:
            moved = None
            for d in range(3):
                for v in range(6):
                    term = jac[d, i, v] * diffs[v][d]
                    moved = term if moved is None else moved + term
            result.append(centres[i] - moved + visc_here * spreads[i])
        return result

    def first_sweep(k):
        for v, val in enumerate(relax(q0, k, 384, range(6))):
            q1[v, k + 1] = jnp.where(inside, val, 0.0)

    for copy in wall_halo:
        copy.wait_recv()
    heard(2, far_sem.at[0])
    pass_on(4, far_sem.at[1])
    rest_halo = halo(WALL, nk)
    for k in range(WALL):
        clean(k)
    for k in range(WALL - 1):
        first_sweep(k)
    wall = relax(q1, 0, 256, [0])[0]
    of_point = (iota((8, 256), 1) & 7) == iota((8, 256), 0)
    spread_wall = jnp.concatenate(
        [jnp.where(of_point, jnp.broadcast_to(wall[2 + i : 3 + i], (8, 256)), 0.0) for i in range(4)],
        axis=1,
    )
    pressure = exact_dot(spread_wall, pick[...], NN_DIMS)
    local_rbf.wait()
    loads = None
    for p in range(8):
        term = rbf_v[p] * pressure[p : p + 1]
        loads = term if loads is None else loads + term
    gap = jnp.zeros((2, 128), F32)
    tall = []
    for k in range(4):
        tall += [loads[k * 6 : k * 6 + 6], gap]
    packed = exact_dot(jnp.concatenate(tall, axis=0), pack[...], NN_DIMS)
    for d in range(ng):
        loads_out[d] = packed[:, d * 128 : (d + 1) * 128]
    load_copies = [send(loads_out.at[d], loads_in.at[d], along_g(d)) for d in range(1, ng)]

    nodes_in[0] = nodes_out[0]
    loads_in[0] = loads_out[0]
    for copy in node_copies:
        copy.wait_recv()
    lane256 = iota((128, 256), 1) + 1
    for d in range(ng):
        upright = jnp.transpose(
            jnp.concatenate([nodes_in[d], jnp.zeros((120, 128), F32)], axis=0)
        ).astype(jnp.int32)
        for k in range(4):
            hit = upright[:, k : k + 1] == lane256
            one_hot[(d * 4 + k) * 128 : (d * 4 + k + 1) * 128, :] = hit.astype(F32).astype(BF16)

    for copy in load_copies:
        copy.wait_recv()
    slot_z = iota((nz, 24, 128), 2) >> bits_cap
    dest_z = (iota((nz, 24, 128), 0) + z) & (nz - 1)
    to_dest = slot_z == dest_z
    for d in range(ng):
        for k in range(4):
            parts = stacked_parts(loads_in[d, k * 8 : k * 8 + 8, :])
            masked = jnp.where(to_dest, jnp.broadcast_to(parts[None], (nz, 24, 128)), 0.0)
            at = (d * 4 + k) * 128
            lhs[:, at : at + 128] = masked.reshape(nz * 24, 128).astype(BF16)
    heard(4, far_sem.at[1])
    dense = jnp.dot(lhs[...], one_hot[...], preferred_element_type=F32)
    largest = functools.reduce(jnp.maximum, [nodes_in[d, 4:5, :] for d in range(ng)])
    largest = jnp.concatenate([largest, largest], axis=1)
    for d in range(nz):
        part_out[d, 6:7, :] = largest
        part = dense[d * 24 : d * 24 + 24]
        part_out[d, 0:6, :] = (part[0:8] + part[8:16] + part[16:24])[0:6]
    part_copies = [
        send(part_out.at[d, 0:7, :], part_in.at[d, 0:7, :], along_z(d)) for d in range(1, nz)
    ]

    for copy in rest_halo:
        copy.wait_recv()

    def clean_loop(k, carry):
        clean(k)
        return carry

    def first_loop(k, carry):
        first_sweep(k)
        return carry

    lax.fori_loop(WALL, nk, clean_loop, 0)
    lax.fori_loop(WALL - 1, nk, first_loop, 0)

    total = part_out[0, 0:6, :]
    for d in range(1, nz):
        part_copies[d - 1].wait_recv()
        total = total + part_in[d, 0:6, :]
        largest = jnp.maximum(largest, part_in[d, 6:7, :])
    scale = 1.0 / largest[:, 0:128]
    force_out[...] = total
    force_copies = {}
    for ob, of in around:
        force_copies[ob, of] = send(force_out, force_in.at[of, ob + REACH], near(ob, of))

    for d in range(ng):
        for k in range(4):
            row = nodes_in[d, k : k + 1, :].astype(jnp.int32)
            hit = row == iota((256, 128), 0) + 1
            at = (d * 4 + k) * 128
            one_hot_t[:, at : at + 128] = hit.astype(F32).astype(BF16)

    for copy in force_copies.values():
        copy.wait_recv()
    for copy in k_copies:
        copy.wait_recv()

    def of_face(ob, df):
        return force_out[...] if (ob, df) == (0, 0) else force_in[df, ob + REACH]

    valid = [(b + p >= 0) & (b + p < nb) for p in range(-REACH, REACH + 1)]
    empty = jnp.zeros((2, 128), F32)
    start = []
    for p in range(-REACH, REACH + 1):
        terms = [of_face(-p, df) for df in range(nf)]
        if nf == 4:
            full = (terms[0] + terms[2]) + (terms[1] + terms[3])
        else:
            full = terms[0] + terms[1]
        full = jnp.where(valid[p + REACH], full, 0.0)
        for half in range(2):
            start.append(jnp.concatenate([full[:, half * 128 : half * 128 + 128], empty], axis=0))
    v0 = dict(enumerate(start))

    reach = [kcols[j, 0] for j in range(8)]
    lane128 = iota((8, 128), 1)

    def times_k(vec, lo, hi):
        shifted = {i: [vec[i]] for i in range(lo, hi)}
        for j in range(1, 7):
            rest = reach[j] % 128
            whole = reach[j] // 128
            back = (128 - rest) % 128
            turned = {i: pltpu.roll(vec[i], back, 1) for i in range(lo - 1, hi + 1)}
            stay = lane128 + rest < 128
            joined = {i: jnp.where(stay, turned[i], turned[i + 1]) for i in range(lo - 1, hi)}
            for i in range(lo, hi):
                far = jnp.where(whole == 1, joined[i], turned[i + 1])
                shifted[i].append(jnp.where(whole == 0, joined[i - 1], far))
        for i in range(lo, hi):
            shifted[i].append(vec[i])
            for j in range(8):
                turn[i, j] = shifted[i][j]
        out = {}
        for i in range(lo, hi):
            lanes = pl.ds((i % 2) * 128, 128)
            columns = [turn[i, :, e, :] for e in range(DOF)]
            rows = []
            for r in range(DOF):
                total = None
                for e in range(DOF):
                    term = kw[i // 2, r, e, :, lanes] * columns[e]
                    total = term if total is None else total + term
                rows.append(jnp.sum(total, axis=0, keepdims=True))
            rows.append(empty)
            out[i] = jnp.where(valid[i // 2], jnp.concatenate(rows, axis=0), 0.0)
        return out

    mid = (2 * REACH, 2 * REACH + 1)

    basis = [v0]
    for n in range(CG_ITERS):
        image = times_k(basis[-1], n + 1, 9 - n)
        fresh = {}
        for i in image:
            turned = 2.0 * (scale * image[i]) - basis[-1][i]
            fresh[i] = turned if n == 0 else 2.0 * turned - basis[-2][i]
        basis.append(fresh)

    row_id, lane_id = iota((8, 128), 0), iota((8, 128), 1)
    pairs = [(i, j) for j in range(CG_ITERS + 1) for i in range(min(j + 1, CG_ITERS))]
    halves = [{i: split(vec[i]) for i in mid} for vec in basis]
    tiles = [(jnp.zeros((8, 128), F32), jnp.zeros((8, 128), F32)) for _ in range(2)]
    for at, (m, n) in enumerate(pairs):
        one, two = [times_exact(basis[m][i], basis[n][i], halves[m][i], halves[n][i]) for i in mid]
        both = add_pairs(one, two)
        for step in (4, 2, 1):
            both = add_pairs(both, (pltpu.roll(both[0], step, 0), pltpu.roll(both[1], step, 0)))
        here = row_id == at % 8
        high, low = tiles[at // 8]
        tiles[at // 8] = (jnp.where(here, both[0], high), jnp.where(here, both[1], low))
    for step in (64, 32, 16, 8, 4, 2, 1):
        tiles = [add_pairs(t, (pltpu.roll(t[0], step, 1), pltpu.roll(t[1], step, 1))) for t in tiles]
    for part in range(2):
        line = sum(
            jnp.sum(jnp.where(lane_id == row_id + 8 * k, tiles[k][part], 0.0), axis=0, keepdims=True)
            for k in range(2)
        )
        dots_a[0, part : part + 1, :] = line
    copies = [send(dots_a.at[0], dots_a.at[d], along_z(d)) for d in range(1, nz)]

    def second_loop(k, carry):
        for v, val in enumerate(relax(q1, k, 256, range(6))):
            q2[v, k] = val
        return carry

    lax.fori_loop(0, nk, second_loop, 0)
    flow_copy = pltpu.make_async_copy(q2.at[:, :, 2:6, :], out_flow, lsem.at[6])
    flow_copy.start()

    for copy in copies:
        copy.wait_recv()
    line = tree([(dots_a[d, 0:1, :], dots_a[d, 1:2, :]) for d in range(nz)])
    for part in range(2):
        dots_b[0, part : part + 1, :] = line[part]
    copies = [send(dots_b.at[0], dots_b.at[d], along_g(d)) for d in range(1, ng)]
    for copy in copies:
        copy.wait_recv()
    line = tree([(dots_b[d, 0:1, :], dots_b[d, 1:2, :]) for d in range(ng)])
    gram = []
    for j in range(CG_ITERS):
        spots = None
        for i in range(CG_ITERS + 1):
            at = pairs.index((min(i, j), max(i, j)))
            spot = (row_id == i) & (lane_id == at)
            spots = spot if spots is None else spots | spot
        column = []
        for part in line:
            picked = jnp.where(spots, jnp.broadcast_to(part, (8, 128)), 0.0)
            column.append(jnp.broadcast_to(jnp.sum(picked, axis=1, keepdims=True), (8, 128)))
        gram.append((column[0], column[1], split(column[0])))

    def entry(vec, j):
        return jnp.broadcast_to(vec[j : j + 1], (8, 128))

    def times_gram(vec, terms):
        total = None
        for j in range(terms):
            by = entry(vec, j)
            high, low = times_exact(gram[j][0], by, gram[j][2], split(by))
            term = (high, low + gram[j][1] * by)
            total = term if total is None else add_pairs(total, term)
        return total[0] + total[1]

    def inner(one, two):
        return jnp.broadcast_to(jnp.sum(one * two, axis=0, keepdims=True), (8, 128))

    def ratio(top, bottom):
        return jnp.where(bottom > 0.0, top / bottom, 0.0)

    def mapped(vec):
        below = pltpu.roll(vec, 1, 0)
        below = jnp.where(row_id == 1, 2.0 * below, below)
        return jnp.where(row_id < 7, 0.5 * vec + 0.25 * (below + pltpu.roll(vec, 7, 0)), 0.0)

    resid = jnp.where(row_id == 0, 1.0, 0.0)
    course = resid
    weights = jnp.zeros((8, 128), F32)
    norm = inner(resid, times_gram(resid, 1))
    for n in range(CG_ITERS):
        moved = mapped(course)
        alpha = ratio(norm, inner(moved, times_gram(course, n + 1)))
        weights = weights + alpha * course
        if n < CG_ITERS - 1:
            resid = resid - alpha * moved
            fresh_norm = jnp.maximum(inner(resid, times_gram(resid, n + 2)), 0.0)
            course = resid + ratio(fresh_norm, norm) * course
            norm = fresh_norm
    answer = []
    for i in mid:
        total = None
        for n in range(CG_ITERS):
            term = entry(weights, n) * basis[n][i]
            total = term if total is None else total + term
        answer.append(scale * total)
    answer = jnp.concatenate(answer, axis=1)
    ans_out[...] = answer
    ans_copies = [
        send(ans_out.at[0:6, :], ans_in.at[d, 0:6, :], along_z(d)) for d in range(1, nz)
    ]
    out_shell[...] = answer[0:6]

    level = []
    zero2 = jnp.zeros((2, 256), F32)
    for d in range(nz):
        if d == 0:
            level.append(stacked_parts(answer))
        else:
            ans_copies[d - 1].wait_recv()
            level.append(stacked_parts(jnp.concatenate([ans_in[d, 0:6, :], zero2], axis=0)))
    wide_x = jnp.concatenate(level, axis=0).astype(BF16)
    from_z = (z + nz - iota((nz, 8, 256), 0)) & (nz - 1)
    from_here = (iota((nz, 8, 256), 2) & 127) >> bits_cap == from_z
    for d in range(ng):
        for k in (0, 2):
            at = (d * 4 + k) * 128
            got = jnp.dot(wide_x, one_hot_t[:, at : at + 256], preferred_element_type=F32)
            got = got.reshape(nz, 3, 8, 256)
            got = got[:, 0] + got[:, 1] + got[:, 2]
            got = jnp.sum(jnp.where(from_here, got, 0.0), axis=0)
            vals_out[d, k * 8 : k * 8 + 8, :] = got[:, 0:128]
            vals_out[d, k * 8 + 8 : k * 8 + 16, :] = got[:, 128:256]
    val_copies = [send(vals_out.at[d], vals_in.at[d], along_g(-d)) for d in range(1, ng)]
    returned = [vals_out[0]]
    for d in range(1, ng):
        val_copies[d - 1].wait_recv()
        returned.append(vals_in[d])
    values = exact_dot(jnp.concatenate(returned, axis=1), pack[...], NT_DIMS)
    values = jnp.concatenate([values[k * 8 : k * 8 + 6] for k in range(4)], axis=0)
    motion = [jnp.sum(rbf_v[p] * values, axis=0, keepdims=True) for p in range(8)]
    out_motion[...] = jnp.concatenate(motion, axis=0)

    flow_copy.wait()
    for copy in sent:
        copy.wait_send()


def hand_over(flow, shell, motion, out_flow, out_shell, out_motion):
    out_flow[...] = flow[...]
    out_shell[...] = shell[...]
    out_motion[...] = motion[...]


def solution(mesh):
    nb, nf = mesh.shape["blk"], mesh.shape["face"]
    ny = 4 if nb == 128 else 2
    nz = nb // (ny * CORES)
    ng = ny * CORES
    count = 8 * 2 + 4 + (ng - 1) * 4 + (nz - 1) * 3 + (5 * nf - 1)

    def local(flow, visc, jac, rbf, cols, owner, kmat, kcols):
        nk = visc.shape[0]
        vmem = pl.BlockSpec(memory_space=pltpu.VMEM)
        smem = pl.BlockSpec(memory_space=pltpu.SMEM)
        hbm = pl.BlockSpec(memory_space=pl.ANY)
        k_total = ng * 512
        scratch = [
            ((7, nk, 8, 256), F32),
            ((7, nk, 8, 128), F32),
            ((7, nk, 8, 128), F32),
            ((7, nk + 2, 8, 384), F32),
            ((6, nk + 2, 8, 384), F32),
            ((6, nk, 8, 256), F32),
            ((8, 24, 128), F32),
            ((5, 6, 6, 8, 256), F32),
            ((1024, 128), BF16),
            ((128, ng * 128), BF16),
            ((ng, 8, 128), F32),
            ((ng, 8, 128), F32),
            ((k_total, 256), BF16),
            ((256, k_total), BF16),
            ((ng, 32, 128), F32),
            ((ng, 32, 128), F32),
            ((nz * 24, k_total), BF16),
            ((nz, 8, 256), F32),
            ((nz, 8, 256), F32),
            ((6, 256), F32),
            ((nf, 5, 6, 256), F32),
            ((nz, 2, 128), F32),
            ((ng, 2, 128), F32),
            ((8, 256), F32),
            ((nz, 8, 256), F32),
            ((ng, 32, 128), F32),
            ((ng, 32, 128), F32),
            ((10, 8, 8, 128), F32),
        ]
        results = pl.pallas_call(
            functools.partial(kernel, ny, nz, nf),
            out_shape=(
                jax.ShapeDtypeStruct(flow.shape, F32),
                jax.ShapeDtypeStruct((6, 256), F32),
                jax.ShapeDtypeStruct((8, 128), F32),
            ),
            in_specs=[hbm, hbm, smem, hbm, vmem, vmem, hbm, smem],
            out_specs=(hbm, vmem, vmem),
            scratch_shapes=[pltpu.VMEM(shape, kind) for shape, kind in scratch]
            + [
                pltpu.SemaphoreType.DMA((count,)),
                pltpu.SemaphoreType.DMA((count,)),
                pltpu.SemaphoreType.DMA((8,)),
                pltpu.SemaphoreType.REGULAR((2,)),
            ],
            compiler_params=pltpu.CompilerParams(
                collective_id=0, has_side_effects=True, vmem_limit_bytes=60 * 1024 * 1024
            ),
        )(flow, visc, jac, rbf, cols, owner.reshape(1, -1), kmat.transpose(1, 2, 0, 3), kcols)
        return pl.pallas_call(
            hand_over,
            out_shape=tuple(jax.ShapeDtypeStruct(r.shape, F32) for r in results),
            in_specs=[vmem] * 3,
            out_specs=(vmem,) * 3,
            compiler_params=pltpu.CompilerParams(vmem_limit_bytes=60 * 1024 * 1024),
        )(*results)

    placed = (
        P(None, None, "blk", "face"),
        P(None, "blk", "face"),
        P(),
        P(None, None, ("blk", "face")),
        P(None, ("blk", "face")),
        P(("blk", "face"), None),
        P(None, None, None, "blk"),
        P(None, "blk"),
    )
    return jax.shard_map(
        local,
        mesh=mesh,
        in_specs=placed,
        out_specs=(P(None, None, "blk", "face"), P(None, "blk"), P(None, ("blk", "face"))),
        check_vma=False,
    )
```

```python
import functools

import jax
import jax.numpy as jnp
from jax import lax
from jax.experimental import pallas as pl
from jax.experimental.pallas import tpu as pltpu
from jax.sharding import PartitionSpec as P

MESH = pl.DeviceIdType.MESH
F32 = jnp.float32
BF16 = jnp.bfloat16
DOF = 6
WALL = 3
CORES = 2
CG_ITERS = 4
REACH = 2


def iota(shape, dim):
    return lax.broadcasted_iota(jnp.int32, shape, dim)


def three_parts(x):
    high = x.astype(BF16).astype(F32)
    rest = x - high
    middle = rest.astype(BF16).astype(F32)
    return high, middle, rest - middle


def stacked_parts(x):
    return jnp.concatenate(three_parts(x), axis=0)


def exact_dot(x, table, dims):
    rows = x.shape[0]
    out = lax.dot_general(
        stacked_parts(x).astype(BF16), table, (dims, ((), ())), preferred_element_type=F32
    )
    return out[:rows] + out[rows : 2 * rows] + out[2 * rows :]


def split(x):
    big = 4097.0 * x
    high = big - (big - x)
    return high, x - high


def times_exact(one, two, one_parts, two_parts):
    (one_h, one_l), (two_h, two_l) = one_parts, two_parts
    high = one * two
    low = ((one_h * two_h - high) + one_h * two_l + one_l * two_h) + one_l * two_l
    return high, low


def add_pairs(one, two):
    total = one[0] + two[0]
    back = total - one[0]
    error = (one[0] - (total - back)) + (two[0] - back)
    return total, one[1] + two[1] + error


def tree(items):
    while len(items) > 1:
        half = len(items) // 2
        items = [add_pairs(items[i], items[i + half]) for i in range(half)]
    return items[0]


NN_DIMS = ((1,), (0,))
NT_DIMS = ((1,), (1,))


def kernel(
    ny, nz, nf,
    flow, visc, jac, rbf, cols, owner, kmat, kcols,
    out_flow, out_shell, out_motion,
    raw, left, right, q0, q1, q2, rbf_v, kw,
    pick, pack, nodes_out, nodes_in, one_hot, one_hot_t, loads_out, loads_in, lhs,
    part_out, part_in, force_out, force_in, dots_a, dots_b,
    ans_out, ans_in, vals_out, vals_in, turn,
    owner_v, cols_v, jac_s, kcols_s, ssem, rsem, lsem, far_sem,
):
    nc = CORES
    ng = ny * nc
    nb = ny * nz * nc
    cap = 128 // nz
    bits_c, bits_z, bits_cap = (n.bit_length() - 1 for n in (nc, nz, cap))
    b = lax.axis_index("blk")
    f = lax.axis_index("face")
    y = b // (nz * nc)
    z = (b // nc) % nz
    c = b % nc
    g = y * nc + c

    def near(ob, of):
        return ((b + ob + nb) % nb, (f + of + nf) % nf)

    def along_g(d):
        other = (g + d + ng) % ng
        return ((other // nc) * (nz * nc) + z * nc + other % nc, f)

    def along_z(d):
        return (y * (nz * nc) + ((z + d + nz) % nz) * nc + c, f)

    used = [0]

    def send(src, dst, to):
        i = used[0]
        used[0] += 1
        copy = pltpu.make_async_remote_copy(
            src_ref=src, dst_ref=dst, send_sem=ssem.at[i], recv_sem=rsem.at[i],
            device_id=to, device_id_type=MESH,
        )
        copy.start()
        sent.append(copy)
        return copy

    sent = []
    nk = visc.shape[0]
    far_first = sorted(range(1, nz), key=lambda d: -min(d, nz - d))

    first_z = (1, 2, nz - 2, nz - 1) if nz > 5 else range(1, nz)
    around = [(ob, of) for of in range(nf) for ob in range(-REACH, REACH + 1) if (ob, of) != (0, 0)]
    peers = [near(ob, of) for ob, of in around]
    peers += [along_g(d) for d in range(1, ng)]
    peers += [along_z(d) for d in first_z]
    barrier = pltpu.get_barrier_semaphore()
    for peer in peers:
        pl.semaphore_signal(barrier, inc=1, device_id=peer, device_id_type=MESH)

    local_wall = [
        pltpu.make_async_copy(flow.at[:, 0:WALL], raw.at[0:6, 0:WALL, 2:6, :], lsem.at[0]),
        pltpu.make_async_copy(visc.at[0:WALL], raw.at[6, 0:WALL, 2:6, :], lsem.at[1]),
    ]
    local_rest = [
        pltpu.make_async_copy(flow.at[:, WALL:nk], raw.at[0:6, WALL:nk, 2:6, :], lsem.at[2]),
        pltpu.make_async_copy(visc.at[WALL:nk], raw.at[6, WALL:nk, 2:6, :], lsem.at[3]),
    ]
    local_k = pltpu.make_async_copy(kmat, kw.at[REACH], lsem.at[4])
    local_rbf = pltpu.make_async_copy(rbf, rbf_v, lsem.at[5])
    small = [
        pltpu.make_async_copy(owner, owner_v, lsem.at[7]),
        pltpu.make_async_copy(cols, cols_v, lsem.at[8]),
        pltpu.make_async_copy(jac, jac_s, lsem.at[9]),
        pltpu.make_async_copy(kcols, kcols_s, lsem.at[10]),
    ]
    for copy in local_wall + small:
        copy.start()
    local_rbf.start()
    for copy in local_rest:
        copy.start()
    local_k.start()

    at_slot = iota((128, 128), 1) - (iota((128, 128), 0) >> 3)
    for i in range(8):
        pick[i * 128 : i * 128 + 128, :] = (at_slot == i * 16).astype(F32).astype(BF16)
    small[0].wait()
    own = jnp.transpose(jnp.broadcast_to(owner_v[...], (128, 128)))[:, 0:1]
    members = (own == iota((128, nb if nb > 128 else 128), 1)).astype(F32)
    earlier = (iota((128, 128), 0) > iota((128, 128), 1)).astype(F32)
    ahead = jnp.dot(earlier.astype(BF16), members.astype(BF16), preferred_element_type=F32)
    rank = jnp.sum(ahead * members, axis=1, keepdims=True).astype(jnp.int32)
    own_c = own & (nc - 1)
    own_z = (own >> bits_c) & (nz - 1)
    own_g = (own >> (bits_c + bits_z)) * nc + own_c
    slot = own_z * cap + rank
    lane = iota((128, 128), 1)
    for d in range(ng):
        here = (own_g == (g + d) % ng) & (slot == lane)
        pack[:, d * 128 : (d + 1) * 128] = here.astype(F32).astype(BF16)
    small[1].wait()
    named = (cols_v[...] + 1).astype(F32)
    named = jnp.concatenate([named, jnp.zeros((4, 128), F32)], axis=0)
    packed_nodes = lax.dot_general(
        named.astype(BF16), pack[...], (NN_DIMS, ((), ())), preferred_element_type=F32
    )
    local_k.wait()
    largest = None
    for r in range(DOF):
        size = sum(jnp.sum(jnp.abs(kw[REACH, r, e]), axis=0, keepdims=True) for e in range(DOF))
        largest = size if largest is None else jnp.maximum(largest, size)
    largest = jnp.broadcast_to(jnp.max(largest, axis=1, keepdims=True), (8, 128))
    node_rows = iota((8, 128), 0) < 4
    for d in range(ng):
        nodes_out[d] = jnp.where(node_rows, packed_nodes[:, d * 128 : (d + 1) * 128], largest)

    pl.semaphore_wait(barrier, len(peers))

    def pass_on(step, sem):
        if nz > 2 * step + 1:
            for d in (step, -step):
                pl.semaphore_signal(sem, inc=1, device_id=along_z(d), device_id_type=MESH)

    def heard(step, sem):
        if nz > 2 * step + 1:
            pl.semaphore_wait(sem, 2)

    pass_on(2, far_sem.at[0])
    small[2].wait()
    small[3].wait()
    for copy in local_wall:
        copy.wait()

    def halo(lo, hi):
        ks = pl.ds(lo, hi - lo)
        low, high = pl.ds(0, 128), pl.ds(128, 128)
        return [
            send(raw.at[:, ks, 4:6, :], raw.at[:, ks, 0:2, :], near(1, 0)),
            send(raw.at[:, ks, 2:4, :], raw.at[:, ks, 6:8, :], near(-1, 0)),
            send(raw.at[:, ks, 2:6, high], left.at[:, ks, 2:6, :], near(0, 1)),
            send(raw.at[:, ks, 2:6, low], right.at[:, ks, 2:6, :], near(0, -1)),
            send(raw.at[:, ks, 5:6, high], left.at[:, ks, 1:2, :], near(1, 1)),
            send(raw.at[:, ks, 5:6, low], right.at[:, ks, 1:2, :], near(1, -1)),
            send(raw.at[:, ks, 2:3, high], left.at[:, ks, 6:7, :], near(-1, 1)),
            send(raw.at[:, ks, 2:3, low], right.at[:, ks, 6:7, :], near(-1, -1)),
        ]

    wall_halo = halo(0, WALL)
    node_copies = [send(nodes_out.at[d], nodes_in.at[d], along_g(d)) for d in range(1, ng)]

    k_copies = [send(kw.at[REACH], kw.at[REACH - o], near(o, 0)) for o in (1, -1)]
    for o, half in ((2, pl.ds(128, 128)), (-2, pl.ds(0, 128))):
        k_copies.append(send(kw.at[REACH, :, :, :, half], kw.at[REACH - o, :, :, :, half], near(o, 0)))
    for copy in local_rest:
        copy.wait()

    row8 = iota((8, 384), 0)
    lane384 = iota((8, 384), 1)
    inside = ((b > 0) | (row8 >= 2)) & ((b < nb - 1) | (row8 < 6))
    inside = inside & ((lane384 < 256) | ((row8 >= 1) & (row8 < 7)))
    inside = inside & ((f < nf - 1) | (lane384 < 256) | (lane384 >= 320))
    inside = inside & ((f > 0) | (lane384 < 320))
    from_right = iota((8, 128), 1) < 64

    zero_plane = jnp.zeros((8, 384), F32)
    for v in range(6):
        for buf in (q0, q1):
            buf[v, 0] = zero_plane
            buf[v, nk + 1] = zero_plane

    def clean(k):
        for v in range(7):
            edge = jnp.where(from_right, right[v, k], left[v, k])
            q0[v, k + 1] = jnp.where(inside, jnp.concatenate([raw[v, k], edge], axis=1), 0.0)

    def relax(src, k, wide, variables):
        diffs = []
        spreads = {}
        centres = {}
        for v in range(6):
            mid = src[v, k + 1]
            trio = [
                (src[v, k + 2, :, 0:wide], src[v, k, :, 0:wide]),
                (pltpu.roll(mid, 7, 0)[:, 0:wide], pltpu.roll(mid, 1, 0)[:, 0:wide]),
                (pltpu.roll(mid, 383, 1)[:, 0:wide], pltpu.roll(mid, 1, 1)[:, 0:wide]),
            ]
            diffs.append([0.5 * (hi - lo) for hi, lo in trio])
            if v in variables:
                centres[v] = mid[:, 0:wide]
                total = -6.0 * centres[v]
                for hi, lo in trio:
                    total = total + hi + lo
                spreads[v] = total
        visc_here = q0[6, k + 1, :, 0:wide]
        result = []
        for i in variables:
            moved = None
            for d in range(3):
                for v in range(6):
                    term = jac_s[d, i, v] * diffs[v][d]
                    moved = term if moved is None else moved + term
            result.append(centres[i] - moved + visc_here * spreads[i])
        return result

    def first_sweep(k):
        for v, val in enumerate(relax(q0, k, 384, range(6))):
            q1[v, k + 1] = jnp.where(inside, val, 0.0)

    for copy in wall_halo:
        copy.wait_recv()
    heard(2, far_sem.at[0])
    pass_on(4, far_sem.at[1])
    rest_halo = halo(WALL, nk)
    for k in range(WALL):
        clean(k)
    for k in range(WALL - 1):
        first_sweep(k)
    wall = relax(q1, 0, 256, [0])[0]
    of_point = (iota((8, 256), 1) & 7) == iota((8, 256), 0)
    spread_wall = jnp.concatenate(
        [jnp.where(of_point, jnp.broadcast_to(wall[2 + i : 3 + i], (8, 256)), 0.0) for i in range(4)],
        axis=1,
    )
    pressure = exact_dot(spread_wall, pick[...], NN_DIMS)
    local_rbf.wait()
    loads = None
    for p in range(8):
        term = rbf_v[p] * pressure[p : p + 1]
        loads = term if loads is None else loads + term
    gap = jnp.zeros((2, 128), F32)
    tall = []
    for k in range(4):
        tall += [loads[k * 6 : k * 6 + 6], gap]
    packed = exact_dot(jnp.concatenate(tall, axis=0), pack[...], NN_DIMS)
    for d in range(ng):
        loads_out[d] = packed[:, d * 128 : (d + 1) * 128]
    load_copies = [send(loads_out.at[d], loads_in.at[d], along_g(d)) for d in range(1, ng)]

    nodes_in[0] = nodes_out[0]
    loads_in[0] = loads_out[0]
    for copy in node_copies:
        copy.wait_recv()
    lane256 = iota((128, 256), 1) + 1
    for d in range(ng):
        upright = jnp.transpose(
            jnp.concatenate([nodes_in[d], jnp.zeros((120, 128), F32)], axis=0)
        ).astype(jnp.int32)
        for k in range(4):
            hit = upright[:, k : k + 1] == lane256
            one_hot[(d * 4 + k) * 128 : (d * 4 + k + 1) * 128, :] = hit.astype(F32).astype(BF16)

    for copy in load_copies:
        copy.wait_recv()
    many = nz // 2
    near_base, far_base = -(nz // 4), many - nz // 4
    slot_z = iota((many, 24, 128), 2) >> bits_cap
    largest = functools.reduce(jnp.maximum, [nodes_in[d, 4:5, :] for d in range(ng)])
    largest = jnp.concatenate([largest, largest], axis=1)
    heard(4, far_sem.at[1])
    part_copies = {}
    for base in (far_base, near_base):
        to_dest = slot_z == (iota((many, 24, 128), 0) + (z + base + nz)) & (nz - 1)
        for d in range(ng):
            for k in range(4):
                parts = stacked_parts(loads_in[d, k * 8 : k * 8 + 8, :])
                masked = jnp.where(to_dest, jnp.broadcast_to(parts[None], (many, 24, 128)), 0.0)
                at = (d * 4 + k) * 128
                lhs[:, at : at + 128] = masked.reshape(many * 24, 128).astype(BF16)
        dense = jnp.dot(lhs[...], one_hot[...], preferred_element_type=F32)
        group = [(i + base) % nz for i in range(many)]
        for i, d in enumerate(group):
            part_out[d, 6:7, :] = largest
            part = dense[i * 24 : i * 24 + 24]
            part_out[d, 0:6, :] = (part[0:8] + part[8:16] + part[16:24])[0:6]
        for d in far_first:
            if d in group:
                part_copies[d] = send(part_out.at[d, 0:7, :], part_in.at[d, 0:7, :], along_z(d))

    for copy in rest_halo:
        copy.wait_recv()

    def clean_loop(k, carry):
        clean(k)
        return carry

    def first_loop(k, carry):
        first_sweep(k)
        return carry

    lax.fori_loop(WALL, nk, clean_loop, 0)
    lax.fori_loop(WALL - 1, nk, first_loop, 0)

    total = part_out[0, 0:6, :]
    for d in range(1, nz):
        part_copies[d].wait_recv()
        total = total + part_in[d, 0:6, :]
        largest = jnp.maximum(largest, part_in[d, 6:7, :])
    scale = 1.0 / largest[:, 0:128]
    force_out[...] = total
    force_copies = {}
    for ob, of in sorted(around, key=lambda p: -min(p[1], nf - p[1]) * 2 - abs(p[0])):
        force_copies[ob, of] = send(force_out, force_in.at[of, ob + REACH], near(ob, of))

    for d in range(ng):
        for k in range(4):
            row = nodes_in[d, k : k + 1, :].astype(jnp.int32)
            hit = row == iota((256, 128), 0) + 1
            at = (d * 4 + k) * 128
            one_hot_t[:, at : at + 128] = hit.astype(F32).astype(BF16)

    for copy in force_copies.values():
        copy.wait_recv()
    for copy in k_copies:
        copy.wait_recv()

    def of_face(ob, df):
        return force_out[...] if (ob, df) == (0, 0) else force_in[df, ob + REACH]

    valid = [(b + p >= 0) & (b + p < nb) for p in range(-REACH, REACH + 1)]
    empty = jnp.zeros((2, 128), F32)
    start = []
    for p in range(-REACH, REACH + 1):
        terms = [of_face(-p, df) for df in range(nf)]
        if nf == 4:
            full = (terms[0] + terms[2]) + (terms[1] + terms[3])
        else:
            full = terms[0] + terms[1]
        full = jnp.where(valid[p + REACH], full, 0.0)
        for half in range(2):
            start.append(jnp.concatenate([full[:, half * 128 : half * 128 + 128], empty], axis=0))
    v0 = dict(enumerate(start))

    reach = [kcols_s[j, 0] for j in range(8)]
    lane128 = iota((8, 128), 1)

    def times_k(vec, lo, hi):
        shifted = {i: [vec[i]] for i in range(lo, hi)}
        for j in range(1, 7):
            rest = reach[j] % 128
            whole = reach[j] // 128
            back = (128 - rest) % 128
            turned = {i: pltpu.roll(vec[i], back, 1) for i in range(lo - 1, hi + 1)}
            stay = lane128 + rest < 128
            joined = {i: jnp.where(stay, turned[i], turned[i + 1]) for i in range(lo - 1, hi)}
            for i in range(lo, hi):
                far = jnp.where(whole == 1, joined[i], turned[i + 1])
                shifted[i].append(jnp.where(whole == 0, joined[i - 1], far))
        for i in range(lo, hi):
            shifted[i].append(vec[i])
            for j in range(8):
                turn[i, j] = shifted[i][j]
        out = {}
        for i in range(lo, hi):
            lanes = pl.ds((i % 2) * 128, 128)
            columns = [turn[i, :, e, :] for e in range(DOF)]
            rows = []
            for r in range(DOF):
                total = None
                for e in range(DOF):
                    term = kw[i // 2, r, e, :, lanes] * columns[e]
                    total = term if total is None else total + term
                rows.append(jnp.sum(total, axis=0, keepdims=True))
            rows.append(empty)
            out[i] = jnp.where(valid[i // 2], jnp.concatenate(rows, axis=0), 0.0)
        return out

    mid = (2 * REACH, 2 * REACH + 1)

    basis = [v0]
    for n in range(CG_ITERS):
        image = times_k(basis[-1], n + 1, 9 - n)
        fresh = {}
        for i in image:
            turned = 2.0 * (scale * image[i]) - basis[-1][i]
            fresh[i] = turned if n == 0 else 2.0 * turned - basis[-2][i]
        basis.append(fresh)

    row_id, lane_id = iota((8, 128), 0), iota((8, 128), 1)
    pairs = [(i, j) for j in range(CG_ITERS + 1) for i in range(min(j + 1, CG_ITERS))]
    halves = [{i: split(vec[i]) for i in mid} for vec in basis]
    tiles = [(jnp.zeros((8, 128), F32), jnp.zeros((8, 128), F32)) for _ in range(2)]
    for at, (m, n) in enumerate(pairs):
        one, two = [times_exact(basis[m][i], basis[n][i], halves[m][i], halves[n][i]) for i in mid]
        both = add_pairs(one, two)
        for step in (4, 2, 1):
            both = add_pairs(both, (pltpu.roll(both[0], step, 0), pltpu.roll(both[1], step, 0)))
        here = row_id == at % 8
        high, low = tiles[at // 8]
        tiles[at // 8] = (jnp.where(here, both[0], high), jnp.where(here, both[1], low))
    for step in (64, 32, 16, 8, 4, 2, 1):
        tiles = [add_pairs(t, (pltpu.roll(t[0], step, 1), pltpu.roll(t[1], step, 1))) for t in tiles]
    for part in range(2):
        line = sum(
            jnp.sum(jnp.where(lane_id == row_id + 8 * k, tiles[k][part], 0.0), axis=0, keepdims=True)
            for k in range(2)
        )
        dots_a[0, part : part + 1, :] = line
    copies = [send(dots_a.at[0], dots_a.at[d], along_z(d)) for d in far_first]

    def second_loop(k, carry):
        for v, val in enumerate(relax(q1, k, 256, range(6))):
            q2[v, k] = val
        return carry

    lax.fori_loop(0, nk, second_loop, 0)
    flow_copy = pltpu.make_async_copy(q2.at[:, :, 2:6, :], out_flow, lsem.at[6])
    flow_copy.start()

    for copy in copies:
        copy.wait_recv()
    line = tree([(dots_a[d, 0:1, :], dots_a[d, 1:2, :]) for d in range(nz)])
    for part in range(2):
        dots_b[0, part : part + 1, :] = line[part]
    copies = [send(dots_b.at[0], dots_b.at[d], along_g(d)) for d in range(1, ng)]
    for copy in copies:
        copy.wait_recv()
    line = tree([(dots_b[d, 0:1, :], dots_b[d, 1:2, :]) for d in range(ng)])
    gram = []
    for j in range(CG_ITERS):
        spots = None
        for i in range(CG_ITERS + 1):
            at = pairs.index((min(i, j), max(i, j)))
            spot = (row_id == i) & (lane_id == at)
            spots = spot if spots is None else spots | spot
        column = []
        for part in line:
            picked = jnp.where(spots, jnp.broadcast_to(part, (8, 128)), 0.0)
            column.append(jnp.broadcast_to(jnp.sum(picked, axis=1, keepdims=True), (8, 128)))
        gram.append((column[0], column[1], split(column[0])))

    def entry(vec, j):
        return jnp.broadcast_to(vec[j : j + 1], (8, 128))

    def times_gram(vec, terms):
        total = None
        for j in range(terms):
            by = entry(vec, j)
            high, low = times_exact(gram[j][0], by, gram[j][2], split(by))
            term = (high, low + gram[j][1] * by)
            total = term if total is None else add_pairs(total, term)
        return total[0] + total[1]

    def inner(one, two):
        return jnp.broadcast_to(jnp.sum(one * two, axis=0, keepdims=True), (8, 128))

    def ratio(top, bottom):
        return jnp.where(bottom > 0.0, top / bottom, 0.0)

    def mapped(vec):
        below = pltpu.roll(vec, 1, 0)
        below = jnp.where(row_id == 1, 2.0 * below, below)
        return jnp.where(row_id < 7, 0.5 * vec + 0.25 * (below + pltpu.roll(vec, 7, 0)), 0.0)

    resid = jnp.where(row_id == 0, 1.0, 0.0)
    course = resid
    weights = jnp.zeros((8, 128), F32)
    norm = inner(resid, times_gram(resid, 1))
    for n in range(CG_ITERS):
        moved = mapped(course)
        alpha = ratio(norm, inner(moved, times_gram(course, n + 1)))
        weights = weights + alpha * course
        if n < CG_ITERS - 1:
            resid = resid - alpha * moved
            fresh_norm = jnp.maximum(inner(resid, times_gram(resid, n + 2)), 0.0)
            course = resid + ratio(fresh_norm, norm) * course
            norm = fresh_norm
    answer = []
    for i in mid:
        total = None
        for n in range(CG_ITERS):
            term = entry(weights, n) * basis[n][i]
            total = term if total is None else total + term
        answer.append(scale * total)
    answer = jnp.concatenate(answer, axis=1)
    ans_out[...] = answer
    ans_copies = {
        d: send(ans_out.at[0:6, :], ans_in.at[d, 0:6, :], along_z(d)) for d in far_first
    }
    flow_copy.wait()
    for copy in sent[:-(nz - 1)]:
        copy.wait_send()
    late = len(sent) - (nz - 1)
    out_shell[...] = answer[0:6]

    zero2 = jnp.zeros((2, 256), F32)
    slot_z = (iota((many, 8, 256), 2) & 127) >> bits_cap
    for base in (near_base, far_base):
        level = []
        for i in range(many):
            d = (i + base) % nz
            if d == 0:
                level.append(stacked_parts(answer))
            else:
                ans_copies[d].wait_recv()
                level.append(stacked_parts(jnp.concatenate([ans_in[d, 0:6, :], zero2], axis=0)))
        wide_x = jnp.concatenate(level, axis=0).astype(BF16)
        from_here = slot_z == (z + 2 * nz - base - iota((many, 8, 256), 0)) & (nz - 1)
        for d in range(ng):
            for k in (0, 2):
                at = (d * 4 + k) * 128
                got = jnp.dot(wide_x, one_hot_t[:, at : at + 256], preferred_element_type=F32)
                got = got.reshape(many, 3, 8, 256)
                got = got[:, 0] + got[:, 1] + got[:, 2]
                got = jnp.sum(jnp.where(from_here, got, 0.0), axis=0)
                for half in range(2):
                    rows = slice((k + half) * 8, (k + half) * 8 + 8)
                    here = got[:, half * 128 : half * 128 + 128]
                    vals_out[d, rows, :] = here if base == near_base else vals_out[d, rows, :] + here
    val_copies = [send(vals_out.at[d], vals_in.at[d], along_g(-d)) for d in range(1, ng)]
    returned = [vals_out[0]]
    for d in range(1, ng):
        val_copies[d - 1].wait_recv()
        returned.append(vals_in[d])
    values = exact_dot(jnp.concatenate(returned, axis=1), pack[...], NT_DIMS)
    values = jnp.concatenate([values[k * 8 : k * 8 + 6] for k in range(4)], axis=0)
    motion = [jnp.sum(rbf_v[p] * values, axis=0, keepdims=True) for p in range(8)]
    out_motion[...] = jnp.concatenate(motion, axis=0)

    for copy in sent[late:]:
        copy.wait_send()


def hand_over(flow, shell, motion, out_flow, out_shell, out_motion):
    out_flow[...] = flow[...]
    out_shell[...] = shell[...]
    out_motion[...] = motion[...]


def solution(mesh):
    nb, nf = mesh.shape["blk"], mesh.shape["face"]
    ny = 4 if nb == 128 else 2
    nz = nb // (ny * CORES)
    ng = ny * CORES
    count = 8 * 2 + 4 + (ng - 1) * 4 + (nz - 1) * 3 + (5 * nf - 1)

    def local(flow, visc, jac, rbf, cols, owner, kmat, kcols):
        nk = visc.shape[0]
        vmem = pl.BlockSpec(memory_space=pltpu.VMEM)
        hbm = pl.BlockSpec(memory_space=pl.ANY)
        k_total = ng * 512
        scratch = [
            ((7, nk, 8, 256), F32),
            ((7, nk, 8, 128), F32),
            ((7, nk, 8, 128), F32),
            ((7, nk + 2, 8, 384), F32),
            ((6, nk + 2, 8, 384), F32),
            ((6, nk, 8, 256), F32),
            ((8, 24, 128), F32),
            ((5, 6, 6, 8, 256), F32),
            ((1024, 128), BF16),
            ((128, ng * 128), BF16),
            ((ng, 8, 128), F32),
            ((ng, 8, 128), F32),
            ((k_total, 256), BF16),
            ((256, k_total), BF16),
            ((ng, 32, 128), F32),
            ((ng, 32, 128), F32),
            ((nz // 2 * 24, k_total), BF16),
            ((nz, 8, 256), F32),
            ((nz, 8, 256), F32),
            ((6, 256), F32),
            ((nf, 5, 6, 256), F32),
            ((nz, 2, 128), F32),
            ((ng, 2, 128), F32),
            ((8, 256), F32),
            ((nz, 8, 256), F32),
            ((ng, 32, 128), F32),
            ((ng, 32, 128), F32),
            ((10, 8, 8, 128), F32),
        ]
        results = pl.pallas_call(
            functools.partial(kernel, ny, nz, nf),
            out_shape=(
                jax.ShapeDtypeStruct(flow.shape, F32),
                jax.ShapeDtypeStruct((6, 256), F32),
                jax.ShapeDtypeStruct((8, 128), F32),
            ),
            in_specs=[hbm] * 8,
            out_specs=(hbm, vmem, vmem),
            scratch_shapes=[pltpu.VMEM(shape, kind) for shape, kind in scratch]
            + [
                pltpu.VMEM((1, 128), jnp.int32),
                pltpu.VMEM((4, 128), jnp.int32),
                pltpu.SMEM((3, 6, 6), F32),
                pltpu.SMEM((8, 256), jnp.int32),
                pltpu.SemaphoreType.DMA((count,)),
                pltpu.SemaphoreType.DMA((count,)),
                pltpu.SemaphoreType.DMA((11,)),
                pltpu.SemaphoreType.REGULAR((2,)),
            ],
            compiler_params=pltpu.CompilerParams(
                collective_id=0, has_side_effects=True, vmem_limit_bytes=60 * 1024 * 1024
            ),
        )(flow, visc, jac, rbf, cols, owner.reshape(1, -1), kmat.transpose(1, 2, 0, 3), kcols)
        return pl.pallas_call(
            hand_over,
            out_shape=tuple(jax.ShapeDtypeStruct(r.shape, F32) for r in results),
            in_specs=[vmem] * 3,
            out_specs=(vmem,) * 3,
            compiler_params=pltpu.CompilerParams(vmem_limit_bytes=60 * 1024 * 1024),
        )(*results)

    placed = (
        P(None, None, "blk", "face"),
        P(None, "blk", "face"),
        P(),
        P(None, None, ("blk", "face")),
        P(None, ("blk", "face")),
        P(("blk", "face"), None),
        P(None, None, None, "blk"),
        P(None, "blk"),
    )
    return jax.shard_map(
        local,
        mesh=mesh,
        in_specs=placed,
        out_specs=(P(None, None, "blk", "face"), P(None, "blk"), P(None, ("blk", "face"))),
        check_vma=False,
    )
```

```python
import functools

import jax
import jax.numpy as jnp
from jax import lax
from jax.experimental import pallas as pl
from jax.experimental.pallas import tpu as pltpu
from jax.sharding import PartitionSpec as P

MESH = pl.DeviceIdType.MESH
F32 = jnp.float32
BF16 = jnp.bfloat16
DOF = 6
WALL = 3
CORES = 2
CG_ITERS = 4
REACH = 2


def iota(shape, dim):
    return lax.broadcasted_iota(jnp.int32, shape, dim)


def three_parts(x):
    high = x.astype(BF16).astype(F32)
    rest = x - high
    middle = rest.astype(BF16).astype(F32)
    return high, middle, rest - middle


def stacked_parts(x):
    return jnp.concatenate(three_parts(x), axis=0)


def exact_dot(x, table, dims):
    rows = x.shape[0]
    out = lax.dot_general(
        stacked_parts(x).astype(BF16), table, (dims, ((), ())), preferred_element_type=F32
    )
    return out[:rows] + out[rows : 2 * rows] + out[2 * rows :]


def split(x):
    big = 4097.0 * x
    high = big - (big - x)
    return high, x - high


def times_exact(one, two, one_parts, two_parts):
    (one_h, one_l), (two_h, two_l) = one_parts, two_parts
    high = one * two
    low = ((one_h * two_h - high) + one_h * two_l + one_l * two_h) + one_l * two_l
    return high, low


def add_pairs(one, two):
    total = one[0] + two[0]
    back = total - one[0]
    error = (one[0] - (total - back)) + (two[0] - back)
    return total, one[1] + two[1] + error


def tree(items):
    while len(items) > 1:
        half = len(items) // 2
        items = [add_pairs(items[i], items[i + half]) for i in range(half)]
    return items[0]


NN_DIMS = ((1,), (0,))
NT_DIMS = ((1,), (1,))


def kernel(
    ny, nz, nf,
    flow, visc, jac, rbf, cols, owner, kmat, kcols,
    out_flow, out_shell, out_motion,
    raw, left, right, q0, q1, q2, rbf_v, kw,
    pick, pack, nodes_out, nodes_in, one_hot, one_hot_t, loads_out, loads_in, lhs,
    part_out, part_in, force_out, force_in, dots_a, dots_b,
    ans_out, ans_in, vals_out, vals_in, turn,
    owner_v, cols_v, jac_s, kcols_s, ssem, rsem, lsem, far_sem,
):
    nc = CORES
    ng = ny * nc
    nb = ny * nz * nc
    cap = 128 // nz
    bits_c, bits_z, bits_cap = (n.bit_length() - 1 for n in (nc, nz, cap))
    b = lax.axis_index("blk")
    f = lax.axis_index("face")
    y = b // (nz * nc)
    z = (b // nc) % nz
    c = b % nc
    g = y * nc + c

    def near(ob, of):
        return ((b + ob + nb) % nb, (f + of + nf) % nf)

    def along_g(d):
        other = (g + d + ng) % ng
        return ((other // nc) * (nz * nc) + z * nc + other % nc, f)

    def along_z(d):
        return (y * (nz * nc) + ((z + d + nz) % nz) * nc + c, f)

    used = [0]

    def send(src, dst, to):
        i = used[0]
        used[0] += 1
        copy = pltpu.make_async_remote_copy(
            src_ref=src, dst_ref=dst, send_sem=ssem.at[i], recv_sem=rsem.at[i],
            device_id=to, device_id_type=MESH,
        )
        copy.start()
        sent.append(copy)
        return copy

    sent = []
    nk = visc.shape[0]
    far_first = sorted(range(1, nz), key=lambda d: -min(d, nz - d))

    first_z = (1, 2, nz - 2, nz - 1) if nz > 5 else range(1, nz)
    around = [(ob, of) for of in range(nf) for ob in range(-REACH, REACH + 1) if (ob, of) != (0, 0)]
    peers = [near(ob, of) for ob, of in around]
    peers += [along_g(d) for d in range(1, ng)]
    peers += [along_z(d) for d in first_z]
    barrier = pltpu.get_barrier_semaphore()
    for peer in peers:
        pl.semaphore_signal(barrier, inc=1, device_id=peer, device_id_type=MESH)

    local_wall = [
        pltpu.make_async_copy(flow.at[:, 0:WALL], raw.at[0:6, 0:WALL, 2:6, :], lsem.at[0]),
        pltpu.make_async_copy(visc.at[0:WALL], raw.at[6, 0:WALL, 2:6, :], lsem.at[1]),
    ]
    local_rest = [
        pltpu.make_async_copy(flow.at[:, WALL:nk], raw.at[0:6, WALL:nk, 2:6, :], lsem.at[2]),
        pltpu.make_async_copy(visc.at[WALL:nk], raw.at[6, WALL:nk, 2:6, :], lsem.at[3]),
    ]
    local_k = pltpu.make_async_copy(kmat, kw.at[REACH], lsem.at[4])
    local_rbf = pltpu.make_async_copy(rbf, rbf_v, lsem.at[5])
    small = [
        pltpu.make_async_copy(owner, owner_v, lsem.at[7]),
        pltpu.make_async_copy(cols, cols_v, lsem.at[8]),
        pltpu.make_async_copy(jac, jac_s, lsem.at[9]),
        pltpu.make_async_copy(kcols, kcols_s, lsem.at[10]),
    ]
    for copy in local_wall + small:
        copy.start()
    local_rbf.start()
    for copy in local_rest:
        copy.start()
    local_k.start()

    at_slot = iota((128, 128), 1) - (iota((128, 128), 0) >> 3)
    for i in range(8):
        pick[i * 128 : i * 128 + 128, :] = (at_slot == i * 16).astype(F32).astype(BF16)
    small[0].wait()
    own = jnp.transpose(jnp.broadcast_to(owner_v[...], (128, 128)))[:, 0:1]
    members = (own == iota((128, nb if nb > 128 else 128), 1)).astype(F32)
    earlier = (iota((128, 128), 0) > iota((128, 128), 1)).astype(F32)
    ahead = jnp.dot(earlier.astype(BF16), members.astype(BF16), preferred_element_type=F32)
    rank = jnp.sum(ahead * members, axis=1, keepdims=True).astype(jnp.int32)
    own_c = own & (nc - 1)
    own_z = (own >> bits_c) & (nz - 1)
    own_g = (own >> (bits_c + bits_z)) * nc + own_c
    slot = own_z * cap + rank
    lane = iota((128, 128), 1)
    for d in range(ng):
        here = (own_g == (g + d) % ng) & (slot == lane)
        pack[:, d * 128 : (d + 1) * 128] = here.astype(F32).astype(BF16)
    small[1].wait()
    named = (cols_v[...] + 1).astype(F32)
    named = jnp.concatenate([named, jnp.zeros((4, 128), F32)], axis=0)
    packed_nodes = lax.dot_general(
        named.astype(BF16), pack[...], (NN_DIMS, ((), ())), preferred_element_type=F32
    )
    local_k.wait()
    largest = None
    for r in range(DOF):
        size = sum(jnp.sum(jnp.abs(kw[REACH, r, e]), axis=0, keepdims=True) for e in range(DOF))
        largest = size if largest is None else jnp.maximum(largest, size)
    largest = jnp.broadcast_to(jnp.max(largest, axis=1, keepdims=True), (8, 128))
    node_rows = iota((8, 128), 0) < 4
    for d in range(ng):
        nodes_out[d] = jnp.where(node_rows, packed_nodes[:, d * 128 : (d + 1) * 128], largest)

    pl.semaphore_wait(barrier, len(peers))

    def pass_on(step, sem):
        if nz > 2 * step + 1:
            for d in (step, -step):
                pl.semaphore_signal(sem, inc=1, device_id=along_z(d), device_id_type=MESH)

    def heard(step, sem):
        if nz > 2 * step + 1:
            pl.semaphore_wait(sem, 2)

    pass_on(2, far_sem.at[0])
    small[2].wait()
    small[3].wait()
    for copy in local_wall:
        copy.wait()

    def halo(lo, hi):
        ks = pl.ds(lo, hi - lo)
        low, high = pl.ds(0, 128), pl.ds(128, 128)
        return [
            send(raw.at[:, ks, 4:6, :], raw.at[:, ks, 0:2, :], near(1, 0)),
            send(raw.at[:, ks, 2:4, :], raw.at[:, ks, 6:8, :], near(-1, 0)),
            send(raw.at[:, ks, 2:6, high], left.at[:, ks, 2:6, :], near(0, 1)),
            send(raw.at[:, ks, 2:6, low], right.at[:, ks, 2:6, :], near(0, -1)),
            send(raw.at[:, ks, 5:6, high], left.at[:, ks, 1:2, :], near(1, 1)),
            send(raw.at[:, ks, 5:6, low], right.at[:, ks, 1:2, :], near(1, -1)),
            send(raw.at[:, ks, 2:3, high], left.at[:, ks, 6:7, :], near(-1, 1)),
            send(raw.at[:, ks, 2:3, low], right.at[:, ks, 6:7, :], near(-1, -1)),
        ]

    wall_halo = halo(0, WALL)
    node_copies = [send(nodes_out.at[d], nodes_in.at[d], along_g(d)) for d in range(1, ng)]

    for copy in local_rest:
        copy.wait()

    row8 = iota((8, 384), 0)
    lane384 = iota((8, 384), 1)
    inside = ((b > 0) | (row8 >= 2)) & ((b < nb - 1) | (row8 < 6))
    inside = inside & ((lane384 < 256) | ((row8 >= 1) & (row8 < 7)))
    inside = inside & ((f < nf - 1) | (lane384 < 256) | (lane384 >= 320))
    inside = inside & ((f > 0) | (lane384 < 320))
    from_right = iota((8, 128), 1) < 64

    zero_plane = jnp.zeros((8, 384), F32)
    for v in range(6):
        for buf in (q0, q1):
            buf[v, 0] = zero_plane
            buf[v, nk + 1] = zero_plane

    def clean(k):
        for v in range(7):
            edge = jnp.where(from_right, right[v, k], left[v, k])
            q0[v, k + 1] = jnp.where(inside, jnp.concatenate([raw[v, k], edge], axis=1), 0.0)

    def relax(src, k, wide, variables):
        diffs = []
        spreads = {}
        centres = {}
        for v in range(6):
            mid = src[v, k + 1]
            trio = [
                (src[v, k + 2, :, 0:wide], src[v, k, :, 0:wide]),
                (pltpu.roll(mid, 7, 0)[:, 0:wide], pltpu.roll(mid, 1, 0)[:, 0:wide]),
                (pltpu.roll(mid, 383, 1)[:, 0:wide], pltpu.roll(mid, 1, 1)[:, 0:wide]),
            ]
            diffs.append([0.5 * (hi - lo) for hi, lo in trio])
            if v in variables:
                centres[v] = mid[:, 0:wide]
                total = -6.0 * centres[v]
                for hi, lo in trio:
                    total = total + hi + lo
                spreads[v] = total
        visc_here = q0[6, k + 1, :, 0:wide]
        result = []
        for i in variables:
            moved = None
            for d in range(3):
                for v in range(6):
                    term = jac_s[d, i, v] * diffs[v][d]
                    moved = term if moved is None else moved + term
            result.append(centres[i] - moved + visc_here * spreads[i])
        return result

    def first_sweep(k):
        for v, val in enumerate(relax(q0, k, 384, range(6))):
            q1[v, k + 1] = jnp.where(inside, val, 0.0)

    for copy in wall_halo:
        copy.wait_recv()
    heard(2, far_sem.at[0])
    pass_on(4, far_sem.at[1])
    rest_halo = halo(WALL, nk)
    for k in range(WALL):
        clean(k)
    for k in range(WALL - 1):
        first_sweep(k)
    wall = relax(q1, 0, 256, [0])[0]
    of_point = (iota((8, 256), 1) & 7) == iota((8, 256), 0)
    spread_wall = jnp.concatenate(
        [jnp.where(of_point, jnp.broadcast_to(wall[2 + i : 3 + i], (8, 256)), 0.0) for i in range(4)],
        axis=1,
    )
    pressure = exact_dot(spread_wall, pick[...], NN_DIMS)
    local_rbf.wait()
    loads = None
    for p in range(8):
        term = rbf_v[p] * pressure[p : p + 1]
        loads = term if loads is None else loads + term
    gap = jnp.zeros((2, 128), F32)
    tall = []
    for k in range(4):
        tall += [loads[k * 6 : k * 6 + 6], gap]
    packed = exact_dot(jnp.concatenate(tall, axis=0), pack[...], NN_DIMS)
    for d in range(ng):
        loads_out[d] = packed[:, d * 128 : (d + 1) * 128]
    load_copies = [send(loads_out.at[d], loads_in.at[d], along_g(d)) for d in range(1, ng)]

    nodes_in[0] = nodes_out[0]
    loads_in[0] = loads_out[0]
    for copy in node_copies:
        copy.wait_recv()
    lane256 = iota((128, 256), 1) + 1
    for d in range(ng):
        upright = jnp.transpose(
            jnp.concatenate([nodes_in[d], jnp.zeros((120, 128), F32)], axis=0)
        ).astype(jnp.int32)
        for k in range(4):
            hit = upright[:, k : k + 1] == lane256
            one_hot[(d * 4 + k) * 128 : (d * 4 + k + 1) * 128, :] = hit.astype(F32).astype(BF16)

    for copy in load_copies:
        copy.wait_recv()
    many = nz // 2
    near_base, far_base = -(nz // 4), many - nz // 4
    slot_z = iota((many, 24, 128), 2) >> bits_cap
    largest = functools.reduce(jnp.maximum, [nodes_in[d, 4:5, :] for d in range(ng)])
    largest = jnp.concatenate([largest, largest], axis=1)
    heard(4, far_sem.at[1])
    part_copies = {}
    for base in (far_base, near_base):
        to_dest = slot_z == (iota((many, 24, 128), 0) + (z + base + nz)) & (nz - 1)
        for d in range(ng):
            for k in range(4):
                parts = stacked_parts(loads_in[d, k * 8 : k * 8 + 8, :])
                masked = jnp.where(to_dest, jnp.broadcast_to(parts[None], (many, 24, 128)), 0.0)
                at = (d * 4 + k) * 128
                lhs[:, at : at + 128] = masked.reshape(many * 24, 128).astype(BF16)
        dense = jnp.dot(lhs[...], one_hot[...], preferred_element_type=F32)
        group = [(i + base) % nz for i in range(many)]
        for i, d in enumerate(group):
            part_out[d, 6:7, :] = largest
            part = dense[i * 24 : i * 24 + 24]
            part_out[d, 0:6, :] = (part[0:8] + part[8:16] + part[16:24])[0:6]
        for d in far_first:
            if d in group:
                part_copies[d] = send(part_out.at[d, 0:7, :], part_in.at[d, 0:7, :], along_z(d))

    k_copies = [send(kw.at[REACH], kw.at[REACH - o], near(o, 0)) for o in (1, -1)]
    for o, half in ((2, pl.ds(128, 128)), (-2, pl.ds(0, 128))):
        k_copies.append(send(kw.at[REACH, :, :, :, half], kw.at[REACH - o, :, :, :, half], near(o, 0)))
    for copy in rest_halo:
        copy.wait_recv()

    def clean_loop(k, carry):
        clean(k)
        return carry

    def first_loop(k, carry):
        first_sweep(k)
        return carry

    lax.fori_loop(WALL, nk, clean_loop, 0)
    lax.fori_loop(WALL - 1, nk, first_loop, 0)

    total = part_out[0, 0:6, :]
    for d in range(1, nz):
        part_copies[d].wait_recv()
        total = total + part_in[d, 0:6, :]
        largest = jnp.maximum(largest, part_in[d, 6:7, :])
    scale = 1.0 / largest[:, 0:128]
    force_out[...] = total
    force_copies = {}
    for ob, of in sorted(around, key=lambda p: -min(p[1], nf - p[1]) * 2 - abs(p[0])):
        force_copies[ob, of] = send(force_out, force_in.at[of, ob + REACH], near(ob, of))

    for d in range(ng):
        for k in range(4):
            row = nodes_in[d, k : k + 1, :].astype(jnp.int32)
            hit = row == iota((256, 128), 0) + 1
            at = (d * 4 + k) * 128
            one_hot_t[:, at : at + 128] = hit.astype(F32).astype(BF16)

    for copy in force_copies.values():
        copy.wait_recv()
    for copy in k_copies:
        copy.wait_recv()

    def of_face(ob, df):
        return force_out[...] if (ob, df) == (0, 0) else force_in[df, ob + REACH]

    valid = [(b + p >= 0) & (b + p < nb) for p in range(-REACH, REACH + 1)]
    empty = jnp.zeros((2, 128), F32)
    start = []
    for p in range(-REACH, REACH + 1):
        terms = [of_face(-p, df) for df in range(nf)]
        if nf == 4:
            full = (terms[0] + terms[2]) + (terms[1] + terms[3])
        else:
            full = terms[0] + terms[1]
        full = jnp.where(valid[p + REACH], full, 0.0)
        for half in range(2):
            start.append(jnp.concatenate([full[:, half * 128 : half * 128 + 128], empty], axis=0))
    v0 = dict(enumerate(start))

    reach = [kcols_s[j, 0] for j in range(8)]
    lane128 = iota((8, 128), 1)

    def times_k(vec, lo, hi):
        shifted = {i: [vec[i]] for i in range(lo, hi)}
        for j in range(1, 7):
            rest = reach[j] % 128
            whole = reach[j] // 128
            back = (128 - rest) % 128
            turned = {i: pltpu.roll(vec[i], back, 1) for i in range(lo - 1, hi + 1)}
            stay = lane128 + rest < 128
            joined = {i: jnp.where(stay, turned[i], turned[i + 1]) for i in range(lo - 1, hi)}
            for i in range(lo, hi):
                far = jnp.where(whole == 1, joined[i], turned[i + 1])
                shifted[i].append(jnp.where(whole == 0, joined[i - 1], far))
        for i in range(lo, hi):
            shifted[i].append(vec[i])
            for j in range(8):
                turn[i, j] = shifted[i][j]
        out = {}
        for i in range(lo, hi):
            lanes = pl.ds((i % 2) * 128, 128)
            columns = [turn[i, :, e, :] for e in range(DOF)]
            rows = []
            for r in range(DOF):
                total = None
                for e in range(DOF):
                    term = kw[i // 2, r, e, :, lanes] * columns[e]
                    total = term if total is None else total + term
                rows.append(jnp.sum(total, axis=0, keepdims=True))
            rows.append(empty)
            out[i] = jnp.where(valid[i // 2], jnp.concatenate(rows, axis=0), 0.0)
        return out

    mid = (2 * REACH, 2 * REACH + 1)

    basis = [v0]
    for n in range(CG_ITERS):
        image = times_k(basis[-1], n + 1, 9 - n)
        fresh = {}
        for i in image:
            turned = 2.0 * (scale * image[i]) - basis[-1][i]
            fresh[i] = turned if n == 0 else 2.0 * turned - basis[-2][i]
        basis.append(fresh)

    row_id, lane_id = iota((8, 128), 0), iota((8, 128), 1)
    pairs = [(i, j) for j in range(CG_ITERS + 1) for i in range(min(j + 1, CG_ITERS))]
    halves = [{i: split(vec[i]) for i in mid} for vec in basis]
    tiles = [(jnp.zeros((8, 128), F32), jnp.zeros((8, 128), F32)) for _ in range(2)]
    for at, (m, n) in enumerate(pairs):
        one, two = [times_exact(basis[m][i], basis[n][i], halves[m][i], halves[n][i]) for i in mid]
        both = add_pairs(one, two)
        for step in (4, 2, 1):
            both = add_pairs(both, (pltpu.roll(both[0], step, 0), pltpu.roll(both[1], step, 0)))
        here = row_id == at % 8
        high, low = tiles[at // 8]
        tiles[at // 8] = (jnp.where(here, both[0], high), jnp.where(here, both[1], low))
    for step in (64, 32, 16, 8, 4, 2, 1):
        tiles = [add_pairs(t, (pltpu.roll(t[0], step, 1), pltpu.roll(t[1], step, 1))) for t in tiles]
    for part in range(2):
        line = sum(
            jnp.sum(jnp.where(lane_id == row_id + 8 * k, tiles[k][part], 0.0), axis=0, keepdims=True)
            for k in range(2)
        )
        dots_a[0, part : part + 1, :] = line
    copies = [send(dots_a.at[0], dots_a.at[d], along_z(d)) for d in far_first]

    def second_loop(k, carry):
        for v, val in enumerate(relax(q1, k, 256, range(6))):
            q2[v, k] = val
        return carry

    lax.fori_loop(0, nk, second_loop, 0)
    flow_copy = pltpu.make_async_copy(q2.at[:, :, 2:6, :], out_flow, lsem.at[6])
    flow_copy.start()

    for copy in copies:
        copy.wait_recv()
    line = tree([(dots_a[d, 0:1, :], dots_a[d, 1:2, :]) for d in range(nz)])
    for part in range(2):
        dots_b[0, part : part + 1, :] = line[part]
    copies = [send(dots_b.at[0], dots_b.at[d], along_g(d)) for d in range(1, ng)]
    for copy in copies:
        copy.wait_recv()
    line = tree([(dots_b[d, 0:1, :], dots_b[d, 1:2, :]) for d in range(ng)])
    gram = []
    for j in range(CG_ITERS):
        spots = None
        for i in range(CG_ITERS + 1):
            at = pairs.index((min(i, j), max(i, j)))
            spot = (row_id == i) & (lane_id == at)
            spots = spot if spots is None else spots | spot
        column = []
        for part in line:
            picked = jnp.where(spots, jnp.broadcast_to(part, (8, 128)), 0.0)
            column.append(jnp.broadcast_to(jnp.sum(picked, axis=1, keepdims=True), (8, 128)))
        gram.append((column[0], column[1], split(column[0])))

    def entry(vec, j):
        return jnp.broadcast_to(vec[j : j + 1], (8, 128))

    def times_gram(vec, terms):
        total = None
        for j in range(terms):
            by = entry(vec, j)
            high, low = times_exact(gram[j][0], by, gram[j][2], split(by))
            term = (high, low + gram[j][1] * by)
            total = term if total is None else add_pairs(total, term)
        return total[0] + total[1]

    def inner(one, two):
        return jnp.broadcast_to(jnp.sum(one * two, axis=0, keepdims=True), (8, 128))

    def ratio(top, bottom):
        return jnp.where(bottom > 0.0, top / bottom, 0.0)

    def mapped(vec):
        below = pltpu.roll(vec, 1, 0)
        below = jnp.where(row_id == 1, 2.0 * below, below)
        return jnp.where(row_id < 7, 0.5 * vec + 0.25 * (below + pltpu.roll(vec, 7, 0)), 0.0)

    resid = jnp.where(row_id == 0, 1.0, 0.0)
    course = resid
    weights = jnp.zeros((8, 128), F32)
    norm = inner(resid, times_gram(resid, 1))
    for n in range(CG_ITERS):
        moved = mapped(course)
        alpha = ratio(norm, inner(moved, times_gram(course, n + 1)))
        weights = weights + alpha * course
        if n < CG_ITERS - 1:
            resid = resid - alpha * moved
            fresh_norm = jnp.maximum(inner(resid, times_gram(resid, n + 2)), 0.0)
            course = resid + ratio(fresh_norm, norm) * course
            norm = fresh_norm
    answer = []
    for i in mid:
        total = None
        for n in range(CG_ITERS):
            term = entry(weights, n) * basis[n][i]
            total = term if total is None else total + term
        answer.append(scale * total)
    answer = jnp.concatenate(answer, axis=1)
    ans_out[...] = answer
    ans_copies = {
        d: send(ans_out.at[0:6, :], ans_in.at[d, 0:6, :], along_z(d)) for d in far_first
    }
    flow_copy.wait()
    for copy in sent[:-(nz - 1)]:
        copy.wait_send()
    late = len(sent) - (nz - 1)
    out_shell[...] = answer[0:6]

    zero2 = jnp.zeros((2, 256), F32)
    slot_z = (iota((many, 8, 256), 2) & 127) >> bits_cap
    for base in (near_base, far_base):
        level = []
        for i in range(many):
            d = (i + base) % nz
            if d == 0:
                level.append(stacked_parts(answer))
            else:
                ans_copies[d].wait_recv()
                level.append(stacked_parts(jnp.concatenate([ans_in[d, 0:6, :], zero2], axis=0)))
        wide_x = jnp.concatenate(level, axis=0).astype(BF16)
        from_here = slot_z == (z + 2 * nz - base - iota((many, 8, 256), 0)) & (nz - 1)
        for d in range(ng):
            for k in (0, 2):
                at = (d * 4 + k) * 128
                got = jnp.dot(wide_x, one_hot_t[:, at : at + 256], preferred_element_type=F32)
                got = got.reshape(many, 3, 8, 256)
                got = got[:, 0] + got[:, 1] + got[:, 2]
                got = jnp.sum(jnp.where(from_here, got, 0.0), axis=0)
                for half in range(2):
                    rows = slice((k + half) * 8, (k + half) * 8 + 8)
                    here = got[:, half * 128 : half * 128 + 128]
                    vals_out[d, rows, :] = here if base == near_base else vals_out[d, rows, :] + here
    val_copies = [send(vals_out.at[d], vals_in.at[d], along_g(-d)) for d in range(1, ng)]
    returned = [vals_out[0]]
    for d in range(1, ng):
        val_copies[d - 1].wait_recv()
        returned.append(vals_in[d])
    values = exact_dot(jnp.concatenate(returned, axis=1), pack[...], NT_DIMS)
    values = jnp.concatenate([values[k * 8 : k * 8 + 6] for k in range(4)], axis=0)
    motion = [jnp.sum(rbf_v[p] * values, axis=0, keepdims=True) for p in range(8)]
    out_motion[...] = jnp.concatenate(motion, axis=0)

    for copy in sent[late:]:
        copy.wait_send()


def hand_over(flow, shell, motion, out_flow, out_shell, out_motion):
    out_flow[...] = flow[...]
    out_shell[...] = shell[...]
    out_motion[...] = motion[...]


def solution(mesh):
    nb, nf = mesh.shape["blk"], mesh.shape["face"]
    ny = 4 if nb == 128 else 2
    nz = nb // (ny * CORES)
    ng = ny * CORES
    count = 8 * 2 + 4 + (ng - 1) * 4 + (nz - 1) * 3 + (5 * nf - 1)

    def local(flow, visc, jac, rbf, cols, owner, kmat, kcols):
        nk = visc.shape[0]
        vmem = pl.BlockSpec(memory_space=pltpu.VMEM)
        hbm = pl.BlockSpec(memory_space=pl.ANY)
        k_total = ng * 512
        scratch = [
            ((7, nk, 8, 256), F32),
            ((7, nk, 8, 128), F32),
            ((7, nk, 8, 128), F32),
            ((7, nk + 2, 8, 384), F32),
            ((6, nk + 2, 8, 384), F32),
            ((6, nk, 8, 256), F32),
            ((8, 24, 128), F32),
            ((5, 6, 6, 8, 256), F32),
            ((1024, 128), BF16),
            ((128, ng * 128), BF16),
            ((ng, 8, 128), F32),
            ((ng, 8, 128), F32),
            ((k_total, 256), BF16),
            ((256, k_total), BF16),
            ((ng, 32, 128), F32),
            ((ng, 32, 128), F32),
            ((nz // 2 * 24, k_total), BF16),
            ((nz, 8, 256), F32),
            ((nz, 8, 256), F32),
            ((6, 256), F32),
            ((nf, 5, 6, 256), F32),
            ((nz, 2, 128), F32),
            ((ng, 2, 128), F32),
            ((8, 256), F32),
            ((nz, 8, 256), F32),
            ((ng, 32, 128), F32),
            ((ng, 32, 128), F32),
            ((10, 8, 8, 128), F32),
        ]
        results = pl.pallas_call(
            functools.partial(kernel, ny, nz, nf),
            out_shape=(
                jax.ShapeDtypeStruct(flow.shape, F32),
                jax.ShapeDtypeStruct((6, 256), F32),
                jax.ShapeDtypeStruct((8, 128), F32),
            ),
            in_specs=[hbm] * 8,
            out_specs=(hbm, vmem, vmem),
            scratch_shapes=[pltpu.VMEM(shape, kind) for shape, kind in scratch]
            + [
                pltpu.VMEM((1, 128), jnp.int32),
                pltpu.VMEM((4, 128), jnp.int32),
                pltpu.SMEM((3, 6, 6), F32),
                pltpu.SMEM((8, 256), jnp.int32),
                pltpu.SemaphoreType.DMA((count,)),
                pltpu.SemaphoreType.DMA((count,)),
                pltpu.SemaphoreType.DMA((11,)),
                pltpu.SemaphoreType.REGULAR((2,)),
            ],
            compiler_params=pltpu.CompilerParams(
                collective_id=0, has_side_effects=True, vmem_limit_bytes=60 * 1024 * 1024
            ),
        )(flow, visc, jac, rbf, cols, owner.reshape(1, -1), kmat.transpose(1, 2, 0, 3), kcols)
        return pl.pallas_call(
            hand_over,
            out_shape=tuple(jax.ShapeDtypeStruct(r.shape, F32) for r in results),
            in_specs=[vmem] * 3,
            out_specs=(vmem,) * 3,
            compiler_params=pltpu.CompilerParams(vmem_limit_bytes=60 * 1024 * 1024),
        )(*results)

    placed = (
        P(None, None, "blk", "face"),
        P(None, "blk", "face"),
        P(),
        P(None, None, ("blk", "face")),
        P(None, ("blk", "face")),
        P(("blk", "face"), None),
        P(None, None, None, "blk"),
        P(None, "blk"),
    )
    return jax.shard_map(
        local,
        mesh=mesh,
        in_specs=placed,
        out_specs=(P(None, None, "blk", "face"), P(None, "blk"), P(None, ("blk", "face"))),
        check_vma=False,
    )
```
